512 devices in a mesh: slab: 4 (over y_lo, core), energy: 128 (over y_hi, z, x).
Axes of the slice: x: 4, y: 8 (y_hi: 4, y_lo: 2; y = y_hi * 2 + y_lo), z: 8, core: 2. Of those that a mesh axis runs over, the one named last changes fastest.
Arguments:
- mode_energy: float32 [2048], replicated, may hold values from -2.5 to 2.5
- levels: int32 [8], P('slab'), may hold values from 0 to 7
- energy_jitter: int32 [256], P('energy'), may hold values from 0 to 7
- offsets: int32 [128], replicated, may hold values from 0 to 255
- scattering: float32 [2, 256, 8, 2048], P(None, 'energy', 'slab'), may hold values from -1.5 to 1.5, as said below
Outputs:
- density: float32 [256, 8, 2048], P('energy', 'slab')
- polarization: float32 [128, 8, 2048], P('energy', 'slab')
The draws below stay inside these ranges and needn't reach their ends.
Inputs may be any that keep to these rules, and one draw needn't show every extreme that they name: scattering[1] (the imaginary part) lies between -0.3 and -0.01; scattering[0] between -1.5 and 1.5.
All inputs are finite; a program needn't handle non-finite values.
Results may differ from the reference program's by a relative error of at most 0.0003.
Values sent between devices are 32-bit elements; how exact they have to be, the bound alone decides.
A program may use at most 64 MiB of HBM per device.

```python
import math
import jax
import jax.numpy as jnp
from jax import lax

MODES = 2048
FINE = 8
EPTS = 256
LAYERS = 8
K = 128


def draw_scattering(key, part):
    key_re, key_im = jax.random.split(jax.random.fold_in(key, 11))
    block_shape = (EPTS, LAYERS, MODES)
    real_part = jnp.clip(0.3 * jax.random.normal(key_re, block_shape, jnp.float32), -1.5, 1.5)
    imag_part = -jnp.exp(jax.random.uniform(key_im, block_shape, jnp.float32, math.log(0.01), math.log(0.3)))
    return jnp.stack((real_part, imag_part)).astype(jnp.float32)


def touch_ends(drawn, key, smallest, top_value):
    longest = drawn.shape.index(max(drawn.shape))
    spots = []
    for shift in (0, 1):
        where = [jax.random.randint(jax.random.fold_in(key, axis), (), 0, length) for axis, length in enumerate(drawn.shape)]
        where[longest] = (where[longest] + shift) % drawn.shape[longest]
        spots.append(tuple(where))
    return drawn.at[spots[0]].set(smallest).at[spots[1]].set(top_value)


def setup_inputs(seed: int = 0) -> dict:
    key_of = jax.random.split(jax.random.key(seed), 6)
    mode_energy = jnp.clip(jax.random.uniform(key_of[0], (MODES,), jnp.float32, -2.5, 2.5), -2.5, 2.5)
    levels = touch_ends(jax.random.randint(key_of[1], (LAYERS,), 0, 8), jax.random.fold_in(key_of[1], 1), 0, 7).astype(jnp.int32)
    energy_jitter = touch_ends(jax.random.randint(key_of[2], (EPTS,), 0, FINE), jax.random.fold_in(key_of[2], 1), 0, FINE - 1).astype(jnp.int32)
    offsets = touch_ends(jax.random.randint(key_of[3], (K,), 0, EPTS), jax.random.fold_in(key_of[3], 1), 0, EPTS - 1).astype(jnp.int32)
    scattering = draw_scattering(jax.random.fold_in(key_of[5], 71), 0)
    return {"mode_energy": mode_energy, "levels": levels, "energy_jitter": energy_jitter, "offsets": offsets, "scattering": scattering}


ETA = 0.1
GAMMA = 0.5
KT = 0.25
STEP_V = 0.15
E_LOW = -3.0
E_SPAN = 6.0


def invert(real_part, imag_part):
    denom = real_part * real_part + imag_part * imag_part
    return real_part / denom, -imag_part / denom


def reference(mode_energy, levels, energy_jitter, offsets, scattering):
    points = energy_jitter.shape[0]
    layer_count = levels.shape[0]
    mode_count = mode_energy.shape[0]
    grid_pos = jnp.arange(points, dtype=jnp.int32)
    energy = E_LOW + E_SPAN * (FINE * grid_pos + energy_jitter).astype(jnp.float32) / (FINE * points)
    potential = STEP_V * levels.astype(jnp.float32)
    a_re = energy[:, None, None] - mode_energy[None, None, :] - potential[None, :, None] - scattering[0]
    a_im = ETA - scattering[1]
    plane = (points, mode_count)
    contact_re = jnp.zeros(plane, jnp.float32)
    contact_im = jnp.full(plane, -GAMMA, jnp.float32)
    left_in = {}
    g_re, g_im = contact_re, contact_im
    for layer in range(layer_count):
        left_in[layer] = (g_re, g_im)
        g_re, g_im = invert(a_re[:, layer] - g_re, a_im[:, layer] - g_im)
    right_in = {}
    g_re, g_im = contact_re, contact_im
    for layer in reversed(range(layer_count)):
        right_in[layer] = (g_re, g_im)
        g_re, g_im = invert(a_re[:, layer] - g_re, a_im[:, layer] - g_im)
    left_re = jnp.stack([left_in[layer][0] for layer in range(layer_count)], axis=1)
    left_im = jnp.stack([left_in[layer][1] for layer in range(layer_count)], axis=1)
    right_re = jnp.stack([right_in[layer][0] for layer in range(layer_count)], axis=1)
    right_im = jnp.stack([right_in[layer][1] for layer in range(layer_count)], axis=1)
    green_re, green_im = invert(a_re - left_re - right_re, a_im - left_im - right_im)
    spectral = -2.0 * green_im
    occupation = 1.0 / (1.0 + jnp.exp(energy / KT))
    density = occupation[:, None, None] * spectral
    hole_part = (1.0 - occupation[:, None, None]) * spectral

    def one_offset(shift_by):
        row_index = ((grid_pos - shift_by) % points).astype(jnp.int32)
        return jnp.sum(density * hole_part[row_index], axis=0) / points

    polarization = lax.map(one_offset, offsets)
    return density, polarization
```

```python
import jax
import jax.numpy as jnp
from jax import lax
from jax.experimental import pallas as pl
from jax.experimental.pallas import tpu as pltpu
from jax.sharding import PartitionSpec as P

FINE = 8
ETA = 0.1
GAMMA = 0.5
KT = 0.25
STEP_V = 0.15
E_LOW = -3.0
E_SPAN = 6.0

SLABS = 4
ENERGY = 128
POINTS = 256
LAYERS = 8
ROW = 4
BLOCKS = ENERGY // ROW
ZS = 8
LOGICAL = pl.DeviceIdType.LOGICAL


def invert(re, im):
    scale = 1.0 / (re * re + im * im)
    return re * scale, -im * scale


def interleave(first, second, odd):
    return (
        jnp.where(odd, pltpu.roll(second, 1, 0), first),
        jnp.where(odd, second, pltpu.roll(first, 7, 0)),
    )


def kernel(
    mode_hbm, levels_hbm, jitter_hbm, offsets_hbm, scat_hbm,
    dens_ref, pol_ref,
    mode, levels, jitter, offsets, scat,
    a_out, a_in, spec, spec_in, en_out, en_in, dens_out, d_all, h_all, pol_out, pol_in,
    load_sem, small_sem, slab_send, slab_recv, en_send, en_recv, spec_send, spec_recv,
    dens_send, dens_recv, pol_send, pol_recv,
):
    s = lax.axis_index("slab")
    e = lax.axis_index("energy")
    r = e // ROW
    x = lax.rem(e, ROW)
    yhi = r // ZS
    z = lax.rem(r, ZS)
    me = s * ENERGY + e

    barrier = pltpu.get_barrier_semaphore()

    def greet(i, carry):
        peer = lax.rem(e + i, ENERGY)
        pl.semaphore_signal(barrier, 1, device_id=s * ENERGY + peer, device_id_type=LOGICAL)
        return carry

    lax.fori_loop(1, ENERGY, greet, 0)
    for i in range(1, SLABS):
        peer = lax.rem(s + i, SLABS)
        pl.semaphore_signal(barrier, 1, device_id=peer * ENERGY + e, device_id_type=LOGICAL)

    def greet_sender(i, carry):
        sender = (i // ZS) * ENERGY + (s * ZS + lax.rem(i, ZS)) * ROW + x

        @pl.when(sender != me)
        def _():
            pl.semaphore_signal(barrier, 1, device_id=sender, device_id_type=LOGICAL)

        return carry

    lax.fori_loop(0, SLABS * ZS, greet_sender, 0)

    loads = [
        pltpu.make_async_copy(scat_hbm, scat, load_sem.at[0]),
        pltpu.make_async_copy(mode_hbm, mode, load_sem.at[1]),
        pltpu.make_async_copy(levels_hbm, levels, small_sem.at[0]),
        pltpu.make_async_copy(jitter_hbm, jitter, small_sem.at[1]),
        pltpu.make_async_copy(offsets_hbm, offsets, small_sem.at[2]),
    ]
    for copy in loads:
        copy.start()
    for copy in loads:
        copy.wait()

    odd = lax.rem(lax.broadcasted_iota(jnp.int32, (8, 128), 0), 2) == 1
    energy = []
    for i in range(2):
        fine = jnp.full((8, 128), FINE * (2 * e + i) + jitter[i], jnp.int32)
        energy.append(E_LOW + E_SPAN * fine.astype(jnp.float32) / (FINE * POINTS))
    level = jnp.where(
        odd, jnp.full((8, 128), levels[1], jnp.int32), jnp.full((8, 128), levels[0], jnp.int32)
    )
    potential = STEP_V * level.astype(jnp.float32)
    for t in range(SLABS):
        modes = jnp.concatenate(
            [jnp.broadcast_to(mode[4 * t + q : 4 * t + q + 1, :], (2, 128)) for q in range(4)], axis=0
        )
        re = [energy[i] - modes - potential - scat[0, i, 8 * t : 8 * t + 8, :] for i in range(2)]
        im = [ETA - scat[1, i, 8 * t : 8 * t + 8, :] for i in range(2)]
        a_out[t, 0, 0], a_out[t, 0, 1] = interleave(re[0], re[1], odd)
        a_out[t, 1, 0], a_out[t, 1, 1] = interleave(im[0], im[1], odd)
    en_out[0:1, :] = energy[0][0:1, :]
    en_out[1:2, :] = energy[1][0:1, :]
    own_energy = jnp.where(odd, energy[1], energy[0])
    own_occ = 1.0 / (1.0 + jnp.exp(own_energy / KT))

    targets = BLOCKS - jnp.where(s == yhi, 1, 0)
    pl.semaphore_wait(barrier, ENERGY - 1 + SLABS - 1 + targets)

    slab_copies = []
    for i in range(1, SLABS):
        peer = lax.rem(s + i, SLABS)
        copy = pltpu.make_async_remote_copy(
            src_ref=a_out.at[peer], dst_ref=a_in.at[s],
            send_sem=slab_send.at[i], recv_sem=slab_recv.at[i],
            device_id=peer * ENERGY + e, device_id_type=LOGICAL,
        )
        copy.start()
        slab_copies.append(copy)
    a_in[s] = a_out[s]

    def send_energy(i, carry):
        peer = lax.rem(e + i, ENERGY)
        pltpu.make_async_remote_copy(
            src_ref=en_out, dst_ref=en_in.at[e], send_sem=en_send, recv_sem=en_recv,
            device_id=s * ENERGY + peer, device_id_type=LOGICAL,
        ).start()
        return carry

    lax.fori_loop(1, ENERGY, send_energy, 0)
    en_in[e] = en_out[...]

    for copy in slab_copies:
        copy.wait_recv()

    a = [(a_in[layer // 2, 0, layer % 2], a_in[layer // 2, 1, layer % 2]) for layer in range(LAYERS)]
    contact = (jnp.zeros((8, 128), jnp.float32), jnp.full((8, 128), -GAMMA, jnp.float32))
    left, right = {}, {}
    g = contact
    for layer in range(LAYERS):
        left[layer] = g
        g = invert(a[layer][0] - g[0], a[layer][1] - g[1])
    g = contact
    for layer in reversed(range(LAYERS)):
        right[layer] = g
        g = invert(a[layer][0] - g[0], a[layer][1] - g[1])
    spectral = []
    for layer in range(LAYERS):
        g = invert(
            a[layer][0] - left[layer][0] - right[layer][0],
            a[layer][1] - left[layer][1] - right[layer][1],
        )
        spectral.append(-2.0 * g[1])
    for layer in range(LAYERS):
        for q in range(4):
            spec[4 * layer + q] = spectral[layer][2 * q : 2 * q + 2, :]

    def send_spec(i, carry):
        peer = lax.rem(e + i, ENERGY)
        pltpu.make_async_remote_copy(
            src_ref=spec.at[peer // ROW], dst_ref=spec_in.at[e], send_sem=spec_send, recv_sem=spec_recv,
            device_id=s * ENERGY + peer, device_id_type=LOGICAL,
        ).start()
        return carry

    lax.fori_loop(1, ENERGY, send_spec, 0)
    spec_in[e] = spec[r]

    for t in range(SLABS):
        first, second = interleave(own_occ * spectral[2 * t], own_occ * spectral[2 * t + 1], odd)
        dens_out[t, 0] = first
        dens_out[t, 1] = second
    dens_copies = []
    for i in range(1, SLABS):
        peer = lax.rem(s + i, SLABS)
        copy = pltpu.make_async_remote_copy(
            src_ref=dens_out.at[peer], dst_ref=dens_ref.at[:, s],
            send_sem=dens_send.at[i], recv_sem=dens_recv.at[i],
            device_id=peer * ENERGY + e, device_id_type=LOGICAL,
        )
        copy.start()
        dens_copies.append(copy)
    dens_ref[:, s] = dens_out[s]

    all_energies = pltpu.make_async_remote_copy(
        src_ref=en_in.at[pl.ds(0, ENERGY - 1)], dst_ref=en_in.at[pl.ds(0, ENERGY - 1)],
        send_sem=en_send, recv_sem=en_recv, device_id=me, device_id_type=LOGICAL,
    )
    all_energies.wait_recv()
    occ_all = 1.0 / (1.0 + jnp.exp(en_in[...].reshape(POINTS, 128) / KT))
    d_all[...] = occ_all

    all_spec = pltpu.make_async_remote_copy(
        src_ref=spec_in.at[pl.ds(0, ENERGY - 1)], dst_ref=spec_in.at[pl.ds(0, ENERGY - 1)],
        send_sem=spec_send, recv_sem=spec_recv, device_id=me, device_id_type=LOGICAL,
    )
    all_spec.wait_recv()
    spec_all = spec_in[...].reshape(POINTS, 128)
    occ_all = d_all[...]
    holes = (1.0 - occ_all) * spec_all
    h_all[0:POINTS, :] = holes
    h_all[POINTS : 2 * POINTS, :] = holes
    d_all[...] = occ_all * spec_all

    slot = (s * 4 + lax.rem(z, 4)) * 2 + z // 4

    def one_offset(i, carry):
        row = lax.rem(r + i, BLOCKS)
        start = POINTS - offsets[row * ROW + x]
        total = jnp.zeros((8, 128), jnp.float32)
        for t in range(POINTS // 8):
            total = total + d_all[8 * t : 8 * t + 8, :] * h_all[pl.ds(start + 8 * t, 8), :]
        pol_out[row] = jnp.sum(total, axis=0, keepdims=True) * (1.0 / POINTS)
        peer = yhi * ENERGY + row * ROW + x

        @pl.when(peer != me)
        def _():
            pltpu.make_async_remote_copy(
                src_ref=pol_out.at[row], dst_ref=pol_in.at[slot], send_sem=pol_send, recv_sem=pol_recv,
                device_id=peer, device_id_type=LOGICAL,
            ).start()

        return carry

    lax.fori_loop(0, BLOCKS, one_offset, 0)

    @pl.when(s == yhi)
    def _():
        pol_in[slot] = pol_out[r]

    def all_pol(count):
        return pltpu.make_async_remote_copy(
            src_ref=pol_in.at[pl.ds(0, count)], dst_ref=pol_in.at[pl.ds(0, count)],
            send_sem=pol_send, recv_sem=pol_recv, device_id=me, device_id_type=LOGICAL,
        )

    for copy in dens_copies:
        copy.wait()
    for copy in slab_copies:
        copy.wait_send()
    all_energies.wait_send()
    all_spec.wait_send()

    @pl.when(s == yhi)
    def _():
        all_pol(BLOCKS - 1).wait()

    @pl.when(s != yhi)
    def _():
        all_pol(BLOCKS).wait()

    for m in range(16):
        for k in range(2):
            pol_ref[m, k : k + 1, :] = pol_in[2 * m + k]


def local(mode_energy, levels, energy_jitter, offsets, scattering):
    modes = mode_energy.reshape(16, 128)
    scat = scattering.reshape(2, 2, 2, 16, 128).transpose(0, 1, 3, 2, 4).reshape(2, 2, 32, 128)
    f32 = jnp.float32
    dma = pltpu.SemaphoreType.DMA
    hbm = pl.BlockSpec(memory_space=pl.ANY)
    vmem = pl.BlockSpec(memory_space=pltpu.VMEM)
    density, polarization = pl.pallas_call(
        kernel,
        out_shape=(
            jax.ShapeDtypeStruct((2, SLABS, 8, 128), f32),
            jax.ShapeDtypeStruct((16, 2, 128), f32),
        ),
        in_specs=[hbm] * 5,
        out_specs=(vmem, vmem),
        scratch_shapes=[
            pltpu.VMEM((16, 128), f32),
            pltpu.SMEM((2,), jnp.int32),
            pltpu.SMEM((2,), jnp.int32),
            pltpu.SMEM((128,), jnp.int32),
            pltpu.VMEM((2, 2, 32, 128), f32),
            pltpu.VMEM((SLABS, 2, 2, 8, 128), f32),
            pltpu.VMEM((SLABS, 2, 2, 8, 128), f32),
            pltpu.VMEM((BLOCKS, 2, 128), f32),
            pltpu.VMEM((ENERGY, 2, 128), f32),
            pltpu.VMEM((2, 128), f32),
            pltpu.VMEM((ENERGY, 2, 128), f32),
            pltpu.VMEM((SLABS, 2, 8, 128), f32),
            pltpu.VMEM((POINTS, 128), f32),
            pltpu.VMEM((2 * POINTS, 128), f32),
            pltpu.VMEM((BLOCKS, 1, 128), f32),
            pltpu.VMEM((BLOCKS, 1, 128), f32),
            dma((2,)),
            dma((3,)),
            dma((SLABS,)),
            dma((SLABS,)),
            dma,
            dma,
            dma,
            dma,
            dma((SLABS,)),
            dma((SLABS,)),
            dma,
            dma,
        ],
        compiler_params=pltpu.CompilerParams(collective_id=0, has_side_effects=True),
        name="green_polarization",
    )(modes, levels, energy_jitter, offsets, scat)
    density = density.reshape(2, 16, 2, 128).transpose(0, 2, 1, 3).reshape(2, 2, 2048)
    polarization = polarization.transpose(1, 0, 2).reshape(1, 2, 2048)
    return density, polarization


def solution(mesh):
    placed = (P(), P("slab"), P("energy"), P(), P(None, "energy", "slab", None))
    return jax.shard_map(
        local,
        mesh=mesh,
        in_specs=placed,
        out_specs=(P("energy", "slab", None), P("energy", "slab", None)),
        check_vma=False,
    )
```

```python
import jax
import jax.numpy as jnp
from jax import lax
from jax.experimental import pallas as pl
from jax.experimental.pallas import tpu as pltpu
from jax.sharding import PartitionSpec as P

FINE = 8
ETA = 0.1
GAMMA = 0.5
KT = 0.25
STEP_V = 0.15
E_LOW = -3.0
E_SPAN = 6.0

SLABS = 4
HUBS = 2
YS, ZS, XS = 4, 8, 4
ENERGY = YS * ZS * XS
ROWS = YS * ZS
POINTS = 256
LAYERS = 8
BLOCKS = 64
SENDERS = 32
LOGICAL = pl.DeviceIdType.LOGICAL


def invert(re, im):
    scale = 1.0 / (re * re + im * im)
    return re * scale, -im * scale


def interleave(first, second, odd):
    return (
        jnp.where(odd, pltpu.roll(second, 1, 0), first),
        jnp.where(odd, second, pltpu.roll(first, 7, 0)),
    )


def far_first(y, z, x):
    ys = [lax.rem(y + d, YS) * (ZS * XS) for d in range(YS)]
    zs = [lax.rem(z + d, ZS) * XS for d in range(ZS)]
    xs = [lax.rem(x + d, XS) for d in range(XS)]
    order = []
    for dy in range(YS):
        for dz in range(ZS):
            for dx in range(XS):
                hops = 2 * min(dy, YS - dy) + min(dz, ZS - dz) + min(dx, XS - dx)
                order.append((-hops, dy, dz, dx))
    order.sort()
    return [ys[dy] + zs[dz] + xs[dx] for hops, dy, dz, dx in order if hops]


def kernel(
    mode_hbm, levels_hbm, jitter_hbm, offsets_hbm, scat_hbm,
    dens_ref, pol_ref,
    mode, levels, jitter, offsets,
    raw_in, lev_out, lev_in, spec, spec_in, en_x, en_row, en_in, dens_out, d_all, h_all, pol_out, pol_in,
    go, load_sem, raw_send, raw_recv, lev_send, lev_recv, x_send, x_recv, en_send, en_recv,
    spec_send, spec_recv, dens_send, dens_recv, pol_send, pol_recv,
):
    s = lax.axis_index("slab")
    e = lax.axis_index("energy")
    y = e // (ZS * XS)
    z = lax.rem(e // XS, ZS)
    x = lax.rem(e, XS)
    me = s * ENERGY + e
    half = 2 * LAYERS

    barrier = pltpu.get_barrier_semaphore()
    level_load = pltpu.make_async_copy(levels_hbm, levels, load_sem.at[0])

    def remote(src, dst, send, recv, device):
        return pltpu.make_async_remote_copy(
            src_ref=src, dst_ref=dst, send_sem=send, recv_sem=recv, device_id=device, device_id_type=LOGICAL
        )

    def raw_copy(hub):
        return remote(
            scat_hbm.at[:, :, pl.ds(half * hub, half), :], raw_in.at[s],
            raw_send.at[hub], raw_recv.at[s], hub * ENERGY + e,
        )

    def lev_copy(hub):
        return remote(lev_out, lev_in.at[s], lev_send.at[hub], lev_recv.at[s], hub * ENERGY + e)

    def load_levels():
        level_load.wait()
        for i in range(2):
            level = jnp.full((1, 128), levels[i], jnp.int32)
            lev_out[i : i + 1, :] = STEP_V * level.astype(jnp.float32)

    def all_pol(count):
        return remote(pol_in.at[pl.ds(0, count)], pol_in.at[pl.ds(0, count)], pol_send, pol_recv, me)

    @pl.when(s >= HUBS)
    def _():
        level_load.start()
        pl.semaphore_wait(barrier, HUBS)
        for hub in range(HUBS):

            @pl.when(s == HUBS)
            def _():
                pl.semaphore_signal(go, 1, device_id=hub * ENERGY + e, device_id_type=LOGICAL)

        for hub in range(HUBS):
            raw_copy(hub).start()
        load_levels()
        for hub in range(HUBS):
            lev_copy(hub).start()
        for hub in range(HUBS):
            raw_copy(hub).wait_send()
            lev_copy(hub).wait_send()
            remote(
                dens_out.at[0], dens_ref.at[:, pl.ds(2 * hub, 2)],
                dens_send.at[0], dens_recv.at[hub], me,
            ).wait_recv()
        all_pol(SENDERS).wait_recv()

    @pl.when(s < HUBS)
    def _():
        other = HUBS - 1 - s
        for leaf in range(HUBS, SLABS):
            pl.semaphore_signal(barrier, 1, device_id=leaf * ENERGY + e, device_id_type=LOGICAL)
        peers = far_first(y, z, x)
        for peer in peers:
            pl.semaphore_signal(barrier, 1, device_id=s * ENERGY + peer, device_id_type=LOGICAL)

        loads = [
            pltpu.make_async_copy(jitter_hbm, jitter, load_sem.at[1]),
            pltpu.make_async_copy(mode_hbm.at[pl.ds(8 * s, 8)], mode, load_sem.at[2]),
            pltpu.make_async_copy(scat_hbm.at[:, :, pl.ds(half * s, half), :], raw_in.at[s], load_sem.at[3]),
            pltpu.make_async_copy(offsets_hbm, offsets, load_sem.at[4]),
        ]
        level_load.start()
        for copy in loads:
            copy.start()
        load_levels()
        lev_in[s] = lev_out[...]
        for copy in loads:
            copy.wait()

        odd = lax.rem(lax.broadcasted_iota(jnp.int32, (8, 128), 0), 2) == 1
        lane = lax.broadcasted_iota(jnp.int32, (8, 128), 1)
        energy = []
        for i in range(2):
            fine = jnp.full((8, 128), FINE * (2 * e + i) + jitter[i], jnp.int32)
            energy.append(E_LOW + E_SPAN * fine.astype(jnp.float32) / (FINE * POINTS))
        own_energy = jnp.where(odd, energy[1], energy[0])
        own_occ = 1.0 / (1.0 + jnp.exp(own_energy / KT))
        place = lane // 16
        mine = jnp.where(place == 2 * x, energy[0], jnp.where(place == 2 * x + 1, energy[1], 0.0))
        en_x[0] = mine[0:1, :]

        pl.semaphore_wait(go, 1)
        raw_copy(other).start()
        lev_copy(other).start()

        def wait_source(source):
            remote(raw_in.at[source], raw_in.at[source], raw_send.at[0], raw_recv.at[source], me).wait_recv()
            remote(lev_out, lev_in.at[source], lev_send.at[0], lev_recv.at[source], me).wait_recv()

        wait_source(other)
        for leaf in range(HUBS, SLABS):
            wait_source(leaf)

        for h in range(2):
            modes = [
                jnp.broadcast_to(mode[4 * h + q : 4 * h + q + 1, :], (2, 128)) for q in range(4)
            ]
            base = own_energy - jnp.concatenate(modes, axis=0)
            a = []
            for source in range(SLABS):
                part = [
                    interleave(
                        raw_in[source, c, 0, 8 * h : 8 * h + 8, :], raw_in[source, c, 1, 8 * h : 8 * h + 8, :], odd
                    )
                    for c in range(2)
                ]
                for k in range(2):
                    a.append((base - lev_in[source, k : k + 1, :] - part[0][k], ETA - part[1][k]))
            contact = (jnp.zeros((8, 128), jnp.float32), jnp.full((8, 128), -GAMMA, jnp.float32))
            left, right = {}, {}
            g = contact
            for layer in range(LAYERS):
                left[layer] = g
                g = invert(a[layer][0] - g[0], a[layer][1] - g[1])
            g = contact
            for layer in reversed(range(LAYERS)):
                right[layer] = g
                g = invert(a[layer][0] - g[0], a[layer][1] - g[1])
            density = []
            for layer in range(LAYERS):
                g = invert(
                    a[layer][0] - left[layer][0] - right[layer][0],
                    a[layer][1] - left[layer][1] - right[layer][1],
                )
                spectral = -2.0 * g[1]
                density.append(own_occ * spectral)
                for q in range(4):
                    spec[8 * layer + 4 * h + q] = spectral[2 * q : 2 * q + 2, :]
            for t in range(SLABS):
                first, second = interleave(density[2 * t], density[2 * t + 1], odd)
                dens_out[t, 0, h] = first
                dens_out[t, 1, h] = second

        pl.semaphore_wait(barrier, ENERGY - 1)
        for i in range(1, XS):
            remote(en_x.at[0], en_x.at[i], x_send, x_recv, me - x + lax.rem(x + i, XS)).start()

        for peer in peers:
            remote(
                spec.at[lax.rem(peer, BLOCKS)], spec_in.at[e], spec_send, spec_recv, s * ENERGY + peer
            ).start()
        block = lax.rem(e, BLOCKS)
        spec_in[e] = spec[block]

        def dens_copy(target):
            return remote(
                dens_out.at[target], dens_ref.at[:, pl.ds(2 * s, 2)],
                dens_send.at[target], dens_recv.at[s], target * ENERGY + e,
            )

        dens_copy(other).start()
        for leaf in range(HUBS, SLABS):
            dens_copy(leaf).start()
        dens_ref[:, pl.ds(2 * s, 2)] = dens_out[s]

        x_all = remote(en_x.at[pl.ds(1, XS - 1)], en_x.at[pl.ds(1, XS - 1)], x_send, x_recv, me)
        x_all.wait()
        en_row[...] = (en_x[0] + en_x[1]) + (en_x[2] + en_x[3])
        row = e // XS
        en_in[row] = en_row[...]
        for i in range(1, ROWS):
            peer = lax.rem(row + i, ROWS)
            remote(en_row, en_in.at[row], en_send, en_recv, s * ENERGY + peer * XS + x).start()
        en_all = remote(en_in.at[pl.ds(0, ROWS - 1)], en_in.at[pl.ds(0, ROWS - 1)], en_send, en_recv, me)
        en_all.wait()
        diagonal = place == lax.broadcasted_iota(jnp.int32, (8, 128), 0)
        for i in range(ROWS):
            spread = jnp.where(diagonal, jnp.broadcast_to(en_in[i], (8, 128)), -100.0)
            column = jnp.broadcast_to(jnp.max(spread, axis=1, keepdims=True), (8, 128))
            d_all[8 * i : 8 * i + 8, :] = 1.0 / (1.0 + jnp.exp(column / KT))

        spec_all = remote(
            spec_in.at[pl.ds(0, ENERGY - 1)], spec_in.at[pl.ds(0, ENERGY - 1)], spec_send, spec_recv, me
        )
        spec_all.wait()
        spectra = spec_in[...].reshape(POINTS, 128)
        occ = d_all[...]
        holes = (1.0 - occ) * spectra
        h_all[0:POINTS, :] = holes
        h_all[POINTS : 2 * POINTS, :] = holes
        d_all[...] = occ * spectra
        d = [d_all[8 * t : 8 * t + 8, :] for t in range(POINTS // 8)]

        first_offset = e - block
        layer = block // 8
        target = layer // 2
        slot = (s * 8 + lax.rem(block, 8)) * 2 + lax.rem(layer, 2)
        own = (target == s).astype(jnp.int32)

        def one_offset(i, carry):
            k = lax.rem(block + 1 + i, BLOCKS)
            start = POINTS - offsets[first_offset + k]
            parts = []
            for t in range(POINTS // 8):
                term = d[t] * h_all[pl.ds(start + 8 * t, 8), :]
                if t < 4:
                    parts.append(term)
                else:
                    parts[t % 4] = parts[t % 4] + term
            total = (parts[0] + parts[1]) + (parts[2] + parts[3])
            pol_out[k] = jnp.sum(total, axis=0, keepdims=True) * (1.0 / POINTS)
            peer = target * ENERGY + first_offset + k

            @pl.when(peer != me)
            def _():
                remote(pol_out.at[k], pol_in.at[slot], pol_send, pol_recv, peer).start()

            return carry

        lax.fori_loop(0, BLOCKS, one_offset, 0)

        @pl.when(own == 1)
        def _():
            pol_in[slot] = pol_out[block]
            remote(
                pol_out.at[pl.ds(0, BLOCKS - 1)], pol_out.at[pl.ds(0, BLOCKS - 1)], pol_send, pol_recv, me
            ).wait_send()
            all_pol(SENDERS - 1).wait_recv()

        @pl.when(own == 0)
        def _():
            remote(pol_out, pol_out, pol_send, pol_recv, me).wait_send()
            all_pol(SENDERS).wait_recv()

        dens_copy(other).wait_send()
        for leaf in range(HUBS, SLABS):
            dens_copy(leaf).wait_send()
        remote(
            dens_out.at[0], dens_ref.at[:, pl.ds(2 * other, 2)], dens_send.at[0], dens_recv.at[other], me
        ).wait_recv()
        raw_copy(other).wait_send()
        lev_copy(other).wait_send()

    for m in range(16):
        for k in range(2):
            pol_ref[m, k : k + 1, :] = pol_in[2 * m + k]


def local(mode_energy, levels, energy_jitter, offsets, scattering):
    modes = mode_energy.reshape(16, 128)
    scat = scattering.reshape(2, 2, 2, 16, 128).transpose(0, 1, 3, 2, 4).reshape(2, 2, 32, 128)
    f32 = jnp.float32
    dma = pltpu.SemaphoreType.DMA
    hbm = pl.BlockSpec(memory_space=pl.ANY)
    vmem = pl.BlockSpec(memory_space=pltpu.VMEM)
    density, polarization = pl.pallas_call(
        kernel,
        out_shape=(
            pltpu.VMEM((2, SLABS, 8, 128), f32),
            pltpu.VMEM((16, 2, 128), f32),
        ),
        in_specs=[hbm] * 5,
        out_specs=(vmem, vmem),
        scratch_shapes=[
            pltpu.VMEM((8, 128), f32),
            pltpu.SMEM((2,), jnp.int32),
            pltpu.SMEM((2,), jnp.int32),
            pltpu.SMEM((128,), jnp.int32),
            pltpu.VMEM((SLABS, 2, 2, 16, 128), f32),
            pltpu.VMEM((2, 128), f32),
            pltpu.VMEM((SLABS, 2, 128), f32),
            pltpu.VMEM((BLOCKS, 2, 128), f32),
            pltpu.VMEM((ENERGY, 2, 128), f32),
            pltpu.VMEM((XS, 1, 128), f32),
            pltpu.VMEM((1, 128), f32),
            pltpu.VMEM((ROWS, 1, 128), f32),
            pltpu.VMEM((SLABS, 2, 2, 8, 128), f32),
            pltpu.VMEM((POINTS, 128), f32),
            pltpu.VMEM((2 * POINTS, 128), f32),
            pltpu.VMEM((BLOCKS, 1, 128), f32),
            pltpu.VMEM((SENDERS, 1, 128), f32),
            pltpu.SemaphoreType.REGULAR,
            dma((5,)),
            dma((HUBS,)),
            dma((SLABS,)),
            dma((HUBS,)),
            dma((SLABS,)),
            dma,
            dma,
            dma,
            dma,
            dma,
            dma,
            dma((SLABS,)),
            dma((HUBS,)),
            dma,
            dma,
        ],
        compiler_params=pltpu.CompilerParams(collective_id=0, has_side_effects=True),
        name="green_polarization",
    )(modes, levels, energy_jitter, offsets, scat)
    density = density.reshape(2, 16, 2, 128).transpose(0, 2, 1, 3).reshape(2, 2, 2048)
    polarization = polarization.transpose(1, 0, 2).reshape(1, 2, 2048)
    return density, polarization


def solution(mesh):
    placed = (P(), P("slab"), P("energy"), P(), P(None, "energy", "slab", None))
    return jax.shard_map(
        local,
        mesh=mesh,
        in_specs=placed,
        out_specs=(P("energy", "slab", None), P("energy", "slab", None)),
        check_vma=False,
    )
```

```python
import jax
import jax.numpy as jnp
from jax import lax
from jax.experimental import pallas as pl
from jax.experimental.pallas import tpu as pltpu
from jax.sharding import PartitionSpec as P

FINE = 8
ETA = 0.1
GAMMA = 0.5
KT = 0.25
STEP_V = 0.15
E_LOW = -3.0
E_SPAN = 6.0

SLABS = 4
HUBS = 2
YS, ZS, XS = 4, 8, 4
ENERGY = YS * ZS * XS
ROWS = YS * ZS
POINTS = 256
LAYERS = 8
BLOCKS = 64
SENDERS = 32
LOGICAL = pl.DeviceIdType.LOGICAL


def times(p, q):
    return p[0] * q[0] - p[1] * q[1], p[0] * q[1] + p[1] * q[0]


def step(a, near, far):
    product = times(a, near)
    return product[0] - far[0], product[1] - far[1]


def interleave(first, second, odd):
    return (
        jnp.where(odd, pltpu.roll(second, 1, 0), first),
        jnp.where(odd, second, pltpu.roll(first, 7, 0)),
    )


def hops_of(dy, dz, dx):
    return 2 * min(dy, YS - dy) + min(dz, ZS - dz) + min(dx, XS - dx)


def far_first(y, z, x):
    ys = [lax.rem(y + d, YS) * (ZS * XS) for d in range(YS)]
    zs = [lax.rem(z + d, ZS) * XS for d in range(ZS)]
    xs = [lax.rem(x + d, XS) for d in range(XS)]
    order = sorted(
        (-hops_of(dy, dz, dx), dy, dz, dx) for dy in range(YS) for dz in range(ZS) for dx in range(XS)
    )
    return [ys[dy] + zs[dz] + xs[dx] for hops, dy, dz, dx in order if hops]


def far_first_of(y, z, x, parity):
    ys = [lax.rem(y + d, YS) * (ZS * XS) for d in range(YS)]
    xs = [lax.rem(x + d, XS) for d in range(XS)]
    same = lax.rem(z, 2) == parity
    steps = ((4, 3), (2, 5), (6, 1), (0, 7))
    zs = [lax.rem(z + jnp.where(same, even, odd), ZS) * XS for even, odd in steps]
    order = sorted(
        (-hops_of(dy, even, dx) - hops_of(dy, odd, dx), dy, n, dx)
        for dy in range(YS)
        for n, (even, odd) in enumerate(steps)
        for dx in range(XS)
    )
    assert order[-1][1:] == (0, 3, 0)
    return [ys[dy] + zs[n] + xs[dx] for hops, dy, n, dx in order]


def kernel(
    mode_hbm, levels_hbm, jitter_hbm, offsets_hbm, scat_hbm,
    dens_ref, pol_ref,
    mode, levels, jitter, offsets,
    raw_in, lev_out, lev_in, spec, spec_in, en_x, en_row, en_in, dens_out, d_all, h_all, pol_out, pol_in,
    go, load_sem, raw_send, raw_recv, lev_send, lev_recv, x_send, x_recv, en_send, en_recv,
    spec_send, spec_recv, dens_send, dens_recv, pol_send, pol_recv,
):
    s = lax.axis_index("slab")
    e = lax.axis_index("energy")
    y = e // (ZS * XS)
    z = lax.rem(e // XS, ZS)
    x = lax.rem(e, XS)
    me = s * ENERGY + e
    half = 16

    barrier = pltpu.get_barrier_semaphore()
    level_load = pltpu.make_async_copy(levels_hbm, levels, load_sem.at[0])

    def remote(src, dst, send, recv, device):
        return pltpu.make_async_remote_copy(
            src_ref=src, dst_ref=dst, send_sem=send, recv_sem=recv, device_id=device, device_id_type=LOGICAL
        )

    def raw_copy(hub, h):
        return remote(
            scat_hbm.at[:, :, pl.ds(half * hub + 8 * h, 8), :], raw_in.at[s, h],
            raw_send.at[hub, h], raw_recv.at[s, h], hub * ENERGY + e,
        )

    def lev_copy(hub):
        return remote(lev_out, lev_in.at[s], lev_send.at[hub], lev_recv.at[s], hub * ENERGY + e)

    def load_levels():
        level_load.wait()
        for i in range(2):
            level = jnp.full((1, 128), levels[i], jnp.int32)
            lev_out[i : i + 1, :] = STEP_V * level.astype(jnp.float32)

    def all_pol(count):
        return remote(pol_in.at[pl.ds(0, count)], pol_in.at[pl.ds(0, count)], pol_send, pol_recv, me)

    @pl.when(s >= HUBS)
    def _():
        level_load.start()
        pl.semaphore_wait(barrier, HUBS)
        for hub in range(HUBS):

            @pl.when(s == HUBS)
            def _():
                pl.semaphore_signal(go, 1, device_id=hub * ENERGY + e, device_id_type=LOGICAL)

        for h in range(2):
            for hub in range(HUBS):
                raw_copy(hub, h).start()
        load_levels()
        for hub in range(HUBS):
            lev_copy(hub).start()
        for hub in range(HUBS):
            for h in range(2):
                raw_copy(hub, h).wait_send()
            lev_copy(hub).wait_send()
            remote(
                dens_out.at[0], dens_ref.at[:, pl.ds(2 * hub, 2)],
                dens_send.at[0], dens_recv.at[hub], me,
            ).wait_recv()
        all_pol(SENDERS).wait_recv()

    @pl.when(s < HUBS)
    def _():
        other = HUBS - 1 - s
        for leaf in range(HUBS, SLABS):
            pl.semaphore_signal(barrier, 1, device_id=leaf * ENERGY + e, device_id_type=LOGICAL)
        peers = far_first(y, z, x)
        for peer in peers:
            pl.semaphore_signal(barrier, 1, device_id=s * ENERGY + peer, device_id_type=LOGICAL)

        loads = [
            pltpu.make_async_copy(jitter_hbm, jitter, load_sem.at[1]),
            pltpu.make_async_copy(mode_hbm.at[pl.ds(8 * s, 8)], mode, load_sem.at[2]),
            pltpu.make_async_copy(offsets_hbm, offsets, load_sem.at[3]),
        ] + [
            pltpu.make_async_copy(
                scat_hbm.at[:, :, pl.ds(half * s + 8 * h, 8), :], raw_in.at[s, h], load_sem.at[4 + h]
            )
            for h in range(2)
        ]
        level_load.start()
        for copy in loads:
            copy.start()
        load_levels()
        lev_in[s] = lev_out[...]
        for copy in loads:
            copy.wait()

        odd = lax.rem(lax.broadcasted_iota(jnp.int32, (8, 128), 0), 2) == 1
        lane = lax.broadcasted_iota(jnp.int32, (8, 128), 1)
        energy = []
        for i in range(2):
            fine = jnp.full((8, 128), FINE * (2 * e + i) + jitter[i], jnp.int32)
            energy.append(E_LOW + E_SPAN * fine.astype(jnp.float32) / (FINE * POINTS))
        own_energy = jnp.where(odd, energy[1], energy[0])
        own_occ = 1.0 / (1.0 + jnp.exp(own_energy / KT))
        place = lane // 16
        mine = jnp.where(place == 2 * x, energy[0], jnp.where(place == 2 * x + 1, energy[1], 0.0))
        en_x[0] = mine[0:1, :]

        pl.semaphore_wait(go, 1)
        for h in range(2):
            raw_copy(other, h).start()
        lev_copy(other).start()

        base = []
        for h in range(2):
            modes = [
                jnp.broadcast_to(mode[4 * h + q : 4 * h + q + 1, :], (2, 128)) for q in range(4)
            ]
            base.append(own_energy - jnp.concatenate(modes, axis=0))

        def wait_levels(source):
            remote(lev_out, lev_in.at[source], lev_send.at[0], lev_recv.at[source], me).wait_recv()

        def wait_raw(source, h):
            remote(
                raw_in.at[source, h], raw_in.at[source, h], raw_send.at[0, 0], raw_recv.at[source, h], me
            ).wait_recv()

        def coefficients(source, h):
            part = [interleave(raw_in[source, h, c, 0], raw_in[source, h, c, 1], odd) for c in range(2)]
            return [
                (base[h] - lev_in[source, k : k + 1, :] - part[0][k], ETA - part[1][k]) for k in range(2)
            ]

        wait_levels(other)
        one = jnp.full((8, 128), 1.0, jnp.float32)
        zero = jnp.zeros((8, 128), jnp.float32)
        contact = (zero, jnp.full((8, 128), -GAMMA, jnp.float32))
        early, theta = [], []
        for h in range(2):
            wait_raw(other, h)
            a = coefficients(0, h) + coefficients(1, h)
            chain = [contact, (one, zero), (a[0][0], a[0][1] + GAMMA)]
            for layer in range(1, 4):
                chain.append(step(a[layer], chain[-1], chain[-2]))
            early.append(a)
            theta.append(chain[1:])

        block = lax.rem(e, BLOCKS)
        for h in range(2):
            for leaf in range(HUBS, SLABS):
                if h == 0:
                    wait_levels(leaf)
                wait_raw(leaf, h)
            a = early[h] + coefficients(2, h) + coefficients(3, h)
            left = list(theta[h])
            for layer in range(4, LAYERS - 1):
                left.append(step(a[layer], left[-1], left[-2]))
            right = [(one, zero), (a[LAYERS - 1][0], a[LAYERS - 1][1] + GAMMA)]
            for layer in reversed(range(1, LAYERS - 1)):
                right.append(step(a[layer], right[-1], right[-2]))
            det = step(a[4], times(left[4], right[3]), times(left[3], right[3]))
            tail = times(left[4], right[2])
            det = (det[0] - tail[0], det[1] - tail[1])
            scale = 2.0 / (det[0] * det[0] + det[1] * det[1])
            weight = (-det[0] * scale, det[1] * scale)
            density = []
            for layer in range(LAYERS):
                product = times(left[layer], right[LAYERS - 1 - layer])
                spectral = product[0] * weight[1] + product[1] * weight[0]
                density.append(own_occ * spectral)
                for q in range(4):
                    spec[8 * layer + 4 * h + q] = spectral[2 * q : 2 * q + 2, :]

            if h == 0:
                pl.semaphore_wait(barrier, ENERGY - 1)
                for i in range(1, XS):
                    remote(en_x.at[0], en_x.at[i], x_send, x_recv, me - x + lax.rem(x + i, XS)).start()

            def send_spec(peer):
                remote(
                    spec.at[lax.rem(peer, BLOCKS)], spec_in.at[e], spec_send, spec_recv, s * ENERGY + peer
                ).start()

            group = far_first_of(y, z, x, h)
            for peer in group[:-1]:
                send_spec(peer)
            nearest = group[-1]

            @pl.when(nearest != e)
            def _():
                send_spec(nearest)

            for t in range(SLABS):
                first, second = interleave(density[2 * t], density[2 * t + 1], odd)
                dens_out[t, 0, h] = first
                dens_out[t, 1, h] = second
        spec_in[e] = spec[block]

        def dens_copy(target):
            return remote(
                dens_out.at[target], dens_ref.at[:, pl.ds(2 * s, 2)],
                dens_send.at[target], dens_recv.at[s], target * ENERGY + e,
            )

        dens_copy(other).start()
        for leaf in range(HUBS, SLABS):
            dens_copy(leaf).start()
        dens_ref[:, pl.ds(2 * s, 2)] = dens_out[s]

        x_all = remote(en_x.at[pl.ds(1, XS - 1)], en_x.at[pl.ds(1, XS - 1)], x_send, x_recv, me)
        x_all.wait()
        en_row[...] = (en_x[0] + en_x[1]) + (en_x[2] + en_x[3])
        row = e // XS
        en_in[row] = en_row[...]
        for i in range(1, ROWS):
            peer = lax.rem(row + i, ROWS)
            remote(en_row, en_in.at[row], en_send, en_recv, s * ENERGY + peer * XS + x).start()
        en_all = remote(en_in.at[pl.ds(0, ROWS - 1)], en_in.at[pl.ds(0, ROWS - 1)], en_send, en_recv, me)
        en_all.wait()
        diagonal = place == lax.broadcasted_iota(jnp.int32, (8, 128), 0)
        for i in range(ROWS):
            spread = jnp.where(diagonal, jnp.broadcast_to(en_in[i], (8, 128)), -100.0)
            column = jnp.broadcast_to(jnp.max(spread, axis=1, keepdims=True), (8, 128))
            d_all[8 * i : 8 * i + 8, :] = 1.0 / (1.0 + jnp.exp(column / KT))

        spec_all = remote(
            spec_in.at[pl.ds(0, ENERGY - 1)], spec_in.at[pl.ds(0, ENERGY - 1)], spec_send, spec_recv, me
        )
        spec_all.wait()
        spectra = spec_in[...].reshape(POINTS, 128)
        occ = d_all[...]
        holes = (1.0 - occ) * spectra
        h_all[0:POINTS, :] = holes
        h_all[POINTS : 2 * POINTS, :] = holes
        d_all[...] = occ * spectra
        d = [d_all[8 * t : 8 * t + 8, :] for t in range(POINTS // 8)]

        first_offset = e - block
        high = lax.rem(y, 2)
        layer = block // 8
        target = layer // 2
        slot = (s * 8 + lax.rem(block, 8)) * 2 + lax.rem(layer, 2)
        own = (target == s).astype(jnp.int32)

        def one_offset(i, carry):
            n = i // 8
            dz = 4 + jnp.where(lax.rem(n, 2) == 1, -((n + 1) // 2), n // 2)
            to_x = lax.rem(x + 2 + lax.rem(i, 4), XS)
            to_y = lax.rem(high + 1 + lax.rem(i, 8) // 4, 2)
            k = to_y * (ZS * XS) + lax.rem(z + dz, ZS) * XS + to_x
            start = POINTS - offsets[first_offset + k]
            parts = []
            for t in range(POINTS // 8):
                term = d[t] * h_all[pl.ds(start + 8 * t, 8), :]
                if t < 4:
                    parts.append(term)
                else:
                    parts[t % 4] = parts[t % 4] + term
            total = (parts[0] + parts[1]) + (parts[2] + parts[3])
            pol_out[k] = jnp.sum(total, axis=0, keepdims=True) * (1.0 / POINTS)
            peer = target * ENERGY + first_offset + k

            @pl.when(peer != me)
            def _():
                remote(pol_out.at[k], pol_in.at[slot], pol_send, pol_recv, peer).start()

            return carry

        lax.fori_loop(0, BLOCKS, one_offset, 0)

        @pl.when(own == 1)
        def _():
            pol_in[slot] = pol_out[block]
            remote(
                pol_out.at[pl.ds(0, BLOCKS - 1)], pol_out.at[pl.ds(0, BLOCKS - 1)], pol_send, pol_recv, me
            ).wait_send()
            all_pol(SENDERS - 1).wait_recv()

        @pl.when(own == 0)
        def _():
            remote(pol_out, pol_out, pol_send, pol_recv, me).wait_send()
            all_pol(SENDERS).wait_recv()

        dens_copy(other).wait_send()
        for leaf in range(HUBS, SLABS):
            dens_copy(leaf).wait_send()
        remote(
            dens_out.at[0], dens_ref.at[:, pl.ds(2 * other, 2)], dens_send.at[0], dens_recv.at[other], me
        ).wait_recv()
        for h in range(2):
            raw_copy(other, h).wait_send()
        lev_copy(other).wait_send()

    for m in range(16):
        for k in range(2):
            pol_ref[m, k : k + 1, :] = pol_in[2 * m + k]


def write_out(dens_ref, pol_ref, dens_hbm, pol_hbm, sem):
    copies = [
        pltpu.make_async_copy(dens_ref, dens_hbm, sem.at[0]),
        pltpu.make_async_copy(pol_ref, pol_hbm, sem.at[1]),
    ]
    for copy in copies:
        copy.start()
    for copy in copies:
        copy.wait()


def local(mode_energy, levels, energy_jitter, offsets, scattering):
    modes = mode_energy.reshape(16, 128)
    scat = scattering.reshape(2, 2, 2, 16, 128).transpose(0, 1, 3, 2, 4).reshape(2, 2, 32, 128)
    f32 = jnp.float32
    dma = pltpu.SemaphoreType.DMA
    hbm = pl.BlockSpec(memory_space=pl.ANY)
    vmem = pl.BlockSpec(memory_space=pltpu.VMEM)
    density, polarization = pl.pallas_call(
        kernel,
        out_shape=(
            pltpu.VMEM((2, SLABS, 8, 128), f32),
            pltpu.VMEM((16, 2, 128), f32),
        ),
        in_specs=[hbm] * 5,
        out_specs=(vmem, vmem),
        scratch_shapes=[
            pltpu.VMEM((8, 128), f32),
            pltpu.SMEM((2,), jnp.int32),
            pltpu.SMEM((2,), jnp.int32),
            pltpu.SMEM((128,), jnp.int32),
            pltpu.VMEM((SLABS, 2, 2, 2, 8, 128), f32),
            pltpu.VMEM((2, 128), f32),
            pltpu.VMEM((SLABS, 2, 128), f32),
            pltpu.VMEM((BLOCKS, 2, 128), f32),
            pltpu.VMEM((ENERGY, 2, 128), f32),
            pltpu.VMEM((XS, 1, 128), f32),
            pltpu.VMEM((1, 128), f32),
            pltpu.VMEM((ROWS, 1, 128), f32),
            pltpu.VMEM((SLABS, 2, 2, 8, 128), f32),
            pltpu.VMEM((POINTS, 128), f32),
            pltpu.VMEM((2 * POINTS, 128), f32),
            pltpu.VMEM((BLOCKS, 1, 128), f32),
            pltpu.VMEM((SENDERS, 1, 128), f32),
            pltpu.SemaphoreType.REGULAR,
            dma((6,)),
            dma((HUBS, 2)),
            dma((SLABS, 2)),
            dma((HUBS,)),
            dma((SLABS,)),
            dma,
            dma,
            dma,
            dma,
            dma,
            dma,
            dma((SLABS,)),
            dma((HUBS,)),
            dma,
            dma,
        ],
        compiler_params=pltpu.CompilerParams(collective_id=0, has_side_effects=True),
        name="green_polarization",
    )(modes, levels, energy_jitter, offsets, scat)
    density, polarization = pl.pallas_call(
        write_out,
        out_shape=(
            jax.ShapeDtypeStruct((2, SLABS, 8, 128), f32),
            jax.ShapeDtypeStruct((16, 2, 128), f32),
        ),
        in_specs=[vmem] * 2,
        out_specs=(hbm, hbm),
        scratch_shapes=[dma((2,))],
        name="write_out",
    )(
        pltpu.with_memory_space_constraint(density, pltpu.VMEM),
        pltpu.with_memory_space_constraint(polarization, pltpu.VMEM),
    )
    density = density.reshape(2, 16, 2, 128).transpose(0, 2, 1, 3).reshape(2, 2, 2048)
    polarization = polarization.transpose(1, 0, 2).reshape(1, 2, 2048)
    return density, polarization


def solution(mesh):
    placed = (P(), P("slab"), P("energy"), P(), P(None, "energy", "slab", None))
    return jax.shard_map(
        local,
        mesh=mesh,
        in_specs=placed,
        out_specs=(P("energy", "slab", None), P("energy", "slab", None)),
        check_vma=False,
    )
```

```python
import jax
import jax.numpy as jnp
from jax import lax
from jax.experimental import pallas as pl
from jax.experimental.pallas import tpu as pltpu
from jax.sharding import PartitionSpec as P

FINE = 8
ETA = 0.1
GAMMA = 0.5
KT = 0.25
STEP_V = 0.15
E_LOW = -3.0
E_SPAN = 6.0

SLABS = 4
HUBS = 2
YS, ZS, XS = 4, 8, 4
ENERGY = YS * ZS * XS
ROWS = YS * ZS
POINTS = 256
LAYERS = 8
BLOCKS = 64
SENDERS = 32
LOGICAL = pl.DeviceIdType.LOGICAL


def times(p, q):
    return p[0] * q[0] - p[1] * q[1], p[0] * q[1] + p[1] * q[0]


def step(a, near, far):
    product = times(a, near)
    return product[0] - far[0], product[1] - far[1]


def interleave(first, second, odd):
    return (
        jnp.where(odd, pltpu.roll(second, 1, 0), first),
        jnp.where(odd, second, pltpu.roll(first, 7, 0)),
    )


def hops_of(dy, dz, dx):
    return 2 * min(dy, YS - dy) + min(dz, ZS - dz) + min(dx, XS - dx)


def far_first(y, z, x):
    ys = [lax.rem(y + d, YS) * (ZS * XS) for d in range(YS)]
    zs = [lax.rem(z + d, ZS) * XS for d in range(ZS)]
    xs = [lax.rem(x + d, XS) for d in range(XS)]
    order = sorted(
        (-hops_of(dy, dz, dx), dy, dz, dx) for dy in range(YS) for dz in range(ZS) for dx in range(XS)
    )
    return [ys[dy] + zs[dz] + xs[dx] for hops, dy, dz, dx in order if hops]


def far_first_of(y, z, x, parity):
    ys = [lax.rem(y + d, YS) * (ZS * XS) for d in range(YS)]
    xs = [lax.rem(x + d, XS) for d in range(XS)]
    same = lax.rem(z, 2) == parity
    steps = ((4, 3), (2, 5), (6, 1), (0, 7))
    zs = [lax.rem(z + jnp.where(same, even, odd), ZS) * XS for even, odd in steps]
    order = sorted(
        (-hops_of(dy, even, dx) - hops_of(dy, odd, dx), dy, n, dx)
        for dy in range(YS)
        for n, (even, odd) in enumerate(steps)
        for dx in range(XS)
    )
    assert order[-1][1:] == (0, 3, 0)
    return [ys[dy] + zs[n] + xs[dx] for hops, dy, n, dx in order]


def kernel(
    mode_hbm, levels_hbm, jitter_hbm, offsets_hbm, scat_hbm,
    dens_ref, pol_ref,
    mode, levels, jitter, offsets,
    raw_in, lev_out, lev_in, spec, spec_in, en_row, en_in, dens_out, d_all, h_all, pol_out, pol_in,
    go, load_sem, raw_send, raw_recv, lev_send, lev_recv, en_send, en_recv,
    spec_send, spec_recv, dens_send, dens_recv, pol_send, pol_recv,
):
    s = lax.axis_index("slab")
    e = lax.axis_index("energy")
    y = e // (ZS * XS)
    z = lax.rem(e // XS, ZS)
    x = lax.rem(e, XS)
    me = s * ENERGY + e
    half = 16

    barrier = pltpu.get_barrier_semaphore()
    level_load = pltpu.make_async_copy(levels_hbm, levels, load_sem.at[0])

    def remote(src, dst, send, recv, device):
        return pltpu.make_async_remote_copy(
            src_ref=src, dst_ref=dst, send_sem=send, recv_sem=recv, device_id=device, device_id_type=LOGICAL
        )

    def raw_copy(hub, h):
        return remote(
            scat_hbm.at[:, :, pl.ds(half * hub + 8 * h, 8), :], raw_in.at[s, h],
            raw_send.at[hub, h], raw_recv.at[s, h], hub * ENERGY + e,
        )

    def lev_copy(hub):
        return remote(lev_out, lev_in.at[s], lev_send.at[hub], lev_recv.at[s], hub * ENERGY + e)

    def load_levels():
        level_load.wait()
        for i in range(2):
            level = jnp.full((1, 128), levels[i], jnp.int32)
            lev_out[i : i + 1, :] = STEP_V * level.astype(jnp.float32)

    def all_pol(count):
        return remote(pol_in.at[pl.ds(0, count)], pol_in.at[pl.ds(0, count)], pol_send, pol_recv, me)

    @pl.when(s >= HUBS)
    def _():
        level_load.start()
        pl.semaphore_wait(barrier, HUBS)
        for hub in range(HUBS):

            @pl.when(s == HUBS)
            def _():
                pl.semaphore_signal(go, 1, device_id=hub * ENERGY + e, device_id_type=LOGICAL)

        for h in range(2):
            for hub in range(HUBS):
                raw_copy(hub, h).start()
        load_levels()
        for hub in range(HUBS):
            lev_copy(hub).start()
        for hub in range(HUBS):
            for h in range(2):
                raw_copy(hub, h).wait_send()
            lev_copy(hub).wait_send()
            remote(
                dens_out.at[0], dens_ref.at[:, pl.ds(2 * hub, 2)],
                dens_send.at[0], dens_recv.at[hub], me,
            ).wait_recv()
        all_pol(SENDERS).wait_recv()

    @pl.when(s < HUBS)
    def _():
        other = HUBS - 1 - s
        for leaf in range(HUBS, SLABS):
            pl.semaphore_signal(barrier, 1, device_id=leaf * ENERGY + e, device_id_type=LOGICAL)
        peers = far_first(y, z, x)
        for peer in peers:
            pl.semaphore_signal(barrier, 1, device_id=s * ENERGY + peer, device_id_type=LOGICAL)

        loads = [
            pltpu.make_async_copy(jitter_hbm, jitter, load_sem.at[1]),
            pltpu.make_async_copy(mode_hbm.at[pl.ds(8 * s, 8)], mode, load_sem.at[2]),
            pltpu.make_async_copy(offsets_hbm, offsets, load_sem.at[3]),
        ] + [
            pltpu.make_async_copy(
                scat_hbm.at[:, :, pl.ds(half * s + 8 * h, 8), :], raw_in.at[s, h], load_sem.at[4 + h]
            )
            for h in range(2)
        ]
        level_load.start()
        for copy in loads:
            copy.start()
        load_levels()
        lev_in[s] = lev_out[...]
        for copy in loads:
            copy.wait()

        odd = lax.rem(lax.broadcasted_iota(jnp.int32, (8, 128), 0), 2) == 1
        lane = lax.broadcasted_iota(jnp.int32, (8, 128), 1)
        energy = []
        for i in range(2):
            fine = jnp.full((8, 128), FINE * (2 * e + i) + jitter[i], jnp.int32)
            energy.append(E_LOW + E_SPAN * fine.astype(jnp.float32) / (FINE * POINTS))
        own_energy = jnp.where(odd, energy[1], energy[0])
        own_occ = 1.0 / (1.0 + jnp.exp(own_energy / KT))
        place = lane // 16
        mine = jnp.where(place == 2 * x, energy[0], jnp.where(place == 2 * x + 1, energy[1], 0.0))
        en_row[...] = mine[0:1, :]

        pl.semaphore_wait(go, 1)
        for h in range(2):
            raw_copy(other, h).start()
        lev_copy(other).start()

        base = []
        for h in range(2):
            modes = [
                jnp.broadcast_to(mode[4 * h + q : 4 * h + q + 1, :], (2, 128)) for q in range(4)
            ]
            base.append(own_energy - jnp.concatenate(modes, axis=0))

        def wait_levels(source):
            remote(lev_out, lev_in.at[source], lev_send.at[0], lev_recv.at[source], me).wait_recv()

        def wait_raw(source, h):
            remote(
                raw_in.at[source, h], raw_in.at[source, h], raw_send.at[0, 0], raw_recv.at[source, h], me
            ).wait_recv()

        def coefficients(source, h):
            part = [interleave(raw_in[source, h, c, 0], raw_in[source, h, c, 1], odd) for c in range(2)]
            return [
                (base[h] - lev_in[source, k : k + 1, :] - part[0][k], ETA - part[1][k]) for k in range(2)
            ]

        wait_levels(other)
        one = jnp.full((8, 128), 1.0, jnp.float32)
        zero = jnp.zeros((8, 128), jnp.float32)
        contact = (zero, jnp.full((8, 128), -GAMMA, jnp.float32))
        early, theta = [], []
        for h in range(2):
            wait_raw(other, h)
            a = coefficients(0, h) + coefficients(1, h)
            chain = [contact, (one, zero), (a[0][0], a[0][1] + GAMMA)]
            for layer in range(1, 4):
                chain.append(step(a[layer], chain[-1], chain[-2]))
            early.append(a)
            theta.append(chain[1:])

        block = lax.rem(e, BLOCKS)
        def send_energies():
            for peer in peers:
                remote(en_row, en_in.at[e], en_send, en_recv, s * ENERGY + peer).start()

        pl.semaphore_wait(barrier, ENERGY - 1)

        @pl.when(s == 0)
        def _():
            send_energies()

        en_in[e] = en_row[...]

        for h in range(2):
            for leaf in range(HUBS, SLABS):
                if h == 0:
                    wait_levels(leaf)
                wait_raw(leaf, h)
            a = early[h] + coefficients(2, h) + coefficients(3, h)
            left = list(theta[h])
            for layer in range(4, LAYERS - 1):
                left.append(step(a[layer], left[-1], left[-2]))
            right = [(one, zero), (a[LAYERS - 1][0], a[LAYERS - 1][1] + GAMMA)]
            for layer in reversed(range(1, LAYERS - 1)):
                right.append(step(a[layer], right[-1], right[-2]))
            det = step(a[4], times(left[4], right[3]), times(left[3], right[3]))
            tail = times(left[4], right[2])
            det = (det[0] - tail[0], det[1] - tail[1])
            scale = 2.0 / (det[0] * det[0] + det[1] * det[1])
            weight = (-det[0] * scale, det[1] * scale)
            density = []
            for layer in range(LAYERS):
                product = times(left[layer], right[LAYERS - 1 - layer])
                spectral = product[0] * weight[1] + product[1] * weight[0]
                density.append(own_occ * spectral)
                for q in range(4):
                    spec[8 * layer + 4 * h + q] = spectral[2 * q : 2 * q + 2, :]


            def send_spec(peer):
                remote(
                    spec.at[lax.rem(peer, BLOCKS)], spec_in.at[e], spec_send, spec_recv, s * ENERGY + peer
                ).start()

            group = far_first_of(y, z, x, h)
            for peer in group[:-1]:
                send_spec(peer)
            nearest = group[-1]

            @pl.when(nearest != e)
            def _():
                send_spec(nearest)

            if h == 1:

                @pl.when(s == 1)
                def _():
                    send_energies()

            for t in range(SLABS):
                first, second = interleave(density[2 * t], density[2 * t + 1], odd)
                dens_out[t, 0, h] = first
                dens_out[t, 1, h] = second
        spec_in[e] = spec[block]

        def dens_copy(target):
            return remote(
                dens_out.at[target], dens_ref.at[:, pl.ds(2 * s, 2)],
                dens_send.at[target], dens_recv.at[s], target * ENERGY + e,
            )

        dens_copy(other).start()
        for leaf in range(HUBS, SLABS):
            dens_copy(leaf).start()
        dens_ref[:, pl.ds(2 * s, 2)] = dens_out[s]

        en_all = remote(en_in.at[pl.ds(0, ENERGY - 1)], en_in.at[pl.ds(0, ENERGY - 1)], en_send, en_recv, me)
        en_all.wait()
        diagonal = place == lax.broadcasted_iota(jnp.int32, (8, 128), 0)
        for i in range(ROWS):
            together = (en_in[4 * i] + en_in[4 * i + 1]) + (en_in[4 * i + 2] + en_in[4 * i + 3])
            spread = jnp.where(diagonal, jnp.broadcast_to(together, (8, 128)), -100.0)
            column = jnp.broadcast_to(jnp.max(spread, axis=1, keepdims=True), (8, 128))
            d_all[8 * i : 8 * i + 8, :] = 1.0 / (1.0 + jnp.exp(column / KT))

        spec_all = remote(
            spec_in.at[pl.ds(0, ENERGY - 1)], spec_in.at[pl.ds(0, ENERGY - 1)], spec_send, spec_recv, me
        )
        spec_all.wait()
        spectra = spec_in[...].reshape(POINTS, 128)
        occ = d_all[...]
        holes = (1.0 - occ) * spectra
        h_all[0:POINTS, :] = holes
        h_all[POINTS : 2 * POINTS, :] = holes
        d_all[...] = occ * spectra
        d = [d_all[8 * t : 8 * t + 8, :] for t in range(POINTS // 8)]

        first_offset = e - block
        high = lax.rem(y, 2)
        layer = block // 8
        target = layer // 2
        slot = (s * 8 + lax.rem(block, 8)) * 2 + lax.rem(layer, 2)
        own = (target == s).astype(jnp.int32)

        def correlate(k):
            start = POINTS - offsets[first_offset + k]
            parts = []
            for t in range(POINTS // 8):
                term = d[t] * h_all[pl.ds(start + 8 * t, 8), :]
                if t < 4:
                    parts.append(term)
                else:
                    parts[t % 4] = parts[t % 4] + term
            total = (parts[0] + parts[1]) + (parts[2] + parts[3])
            pol_out[k] = jnp.sum(total, axis=0, keepdims=True) * (1.0 / POINTS)

        def give(k):
            peer = target * ENERGY + first_offset + k
            remote(pol_out.at[k], pol_in.at[slot], pol_send, pol_recv, peer).start()

        def one_offset(i, carry):
            k = lax.rem(block + 1 + i, BLOCKS)
            correlate(k)
            give(k)
            return carry

        lax.fori_loop(0, BLOCKS - 1, one_offset, 0, unroll=3)
        correlate(block)

        @pl.when(own == 0)
        def _():
            give(block)

        @pl.when(own == 1)
        def _():
            pol_in[slot] = pol_out[block]
            remote(
                pol_out.at[pl.ds(0, BLOCKS - 1)], pol_out.at[pl.ds(0, BLOCKS - 1)], pol_send, pol_recv, me
            ).wait_send()
            all_pol(SENDERS - 1).wait_recv()

        @pl.when(own == 0)
        def _():
            remote(pol_out, pol_out, pol_send, pol_recv, me).wait_send()
            all_pol(SENDERS).wait_recv()

        dens_copy(other).wait_send()
        for leaf in range(HUBS, SLABS):
            dens_copy(leaf).wait_send()
        remote(
            dens_out.at[0], dens_ref.at[:, pl.ds(2 * other, 2)], dens_send.at[0], dens_recv.at[other], me
        ).wait_recv()
        for h in range(2):
            raw_copy(other, h).wait_send()
        lev_copy(other).wait_send()

    for m in range(16):
        for k in range(2):
            pol_ref[m, k : k + 1, :] = pol_in[2 * m + k]


def write_out(dens_ref, pol_ref, dens_hbm, pol_hbm, sem):
    copies = [
        pltpu.make_async_copy(dens_ref, dens_hbm, sem.at[0]),
        pltpu.make_async_copy(pol_ref, pol_hbm, sem.at[1]),
    ]
    for copy in copies:
        copy.start()
    for copy in copies:
        copy.wait()


def local(mode_energy, levels, energy_jitter, offsets, scattering):
    modes = mode_energy.reshape(16, 128)
    scat = scattering.reshape(2, 2, 2, 16, 128).transpose(0, 1, 3, 2, 4).reshape(2, 2, 32, 128)
    f32 = jnp.float32
    dma = pltpu.SemaphoreType.DMA
    hbm = pl.BlockSpec(memory_space=pl.ANY)
    vmem = pl.BlockSpec(memory_space=pltpu.VMEM)
    density, polarization = pl.pallas_call(
        kernel,
        out_shape=(
            pltpu.VMEM((2, SLABS, 8, 128), f32),
            pltpu.VMEM((16, 2, 128), f32),
        ),
        in_specs=[hbm] * 5,
        out_specs=(vmem, vmem),
        scratch_shapes=[
            pltpu.VMEM((8, 128), f32),
            pltpu.SMEM((2,), jnp.int32),
            pltpu.SMEM((2,), jnp.int32),
            pltpu.SMEM((128,), jnp.int32),
            pltpu.VMEM((SLABS, 2, 2, 2, 8, 128), f32),
            pltpu.VMEM((2, 128), f32),
            pltpu.VMEM((SLABS, 2, 128), f32),
            pltpu.VMEM((BLOCKS, 2, 128), f32),
            pltpu.VMEM((ENERGY, 2, 128), f32),
            pltpu.VMEM((1, 128), f32),
            pltpu.VMEM((ENERGY, 1, 128), f32),
            pltpu.VMEM((SLABS, 2, 2, 8, 128), f32),
            pltpu.VMEM((POINTS, 128), f32),
            pltpu.VMEM((2 * POINTS, 128), f32),
            pltpu.VMEM((BLOCKS, 1, 128), f32),
            pltpu.VMEM((SENDERS, 1, 128), f32),
            pltpu.SemaphoreType.REGULAR,
            dma((6,)),
            dma((HUBS, 2)),
            dma((SLABS, 2)),
            dma((HUBS,)),
            dma((SLABS,)),
            dma,
            dma,
            dma,
            dma,
            dma((SLABS,)),
            dma((HUBS,)),
            dma,
            dma,
        ],
        compiler_params=pltpu.CompilerParams(collective_id=0, has_side_effects=True),
        name="green_polarization",
    )(modes, levels, energy_jitter, offsets, scat)
    density, polarization = pl.pallas_call(
        write_out,
        out_shape=(
            jax.ShapeDtypeStruct((2, SLABS, 8, 128), f32),
            jax.ShapeDtypeStruct((16, 2, 128), f32),
        ),
        in_specs=[vmem] * 2,
        out_specs=(hbm, hbm),
        scratch_shapes=[dma((2,))],
        name="write_out",
    )(
        pltpu.with_memory_space_constraint(density, pltpu.VMEM),
        pltpu.with_memory_space_constraint(polarization, pltpu.VMEM),
    )
    density = density.reshape(2, 16, 2, 128).transpose(0, 2, 1, 3).reshape(2, 2, 2048)
    polarization = polarization.transpose(1, 0, 2).reshape(1, 2, 2048)
    return density, polarization


def solution(mesh):
    placed = (P(), P("slab"), P("energy"), P(), P(None, "energy", "slab", None))
    return jax.shard_map(
        local,
        mesh=mesh,
        in_specs=placed,
        out_specs=(P("energy", "slab", None), P("energy", "slab", None)),
        check_vma=False,
    )
```

```python
import jax
import jax.numpy as jnp
from jax import lax
from jax.experimental import pallas as pl
from jax.experimental.pallas import tpu as pltpu
from jax.sharding import PartitionSpec as P

FINE = 8
ETA = 0.1
GAMMA = 0.5
KT = 0.25
STEP_V = 0.15
E_LOW = -3.0
E_SPAN = 6.0

SLABS = 4
HUBS = 2
YS, ZS, XS = 4, 8, 4
ENERGY = YS * ZS * XS
ROWS = YS * ZS
POINTS = 256
LAYERS = 8
BLOCKS = 64
SENDERS = 32
LOGICAL = pl.DeviceIdType.LOGICAL


def times(p, q):
    return p[0] * q[0] - p[1] * q[1], p[0] * q[1] + p[1] * q[0]


def step(a, near, far):
    product = times(a, near)
    return product[0] - far[0], product[1] - far[1]


def interleave(first, second, odd):
    return (
        jnp.where(odd, pltpu.roll(second, 1, 0), first),
        jnp.where(odd, second, pltpu.roll(first, 7, 0)),
    )


def hops_of(dy, dz, dx):
    return 2 * min(dy, YS - dy) + min(dz, ZS - dz) + min(dx, XS - dx)


def far_first(y, z, x):
    ys = [lax.rem(y + d, YS) * (ZS * XS) for d in range(YS)]
    zs = [lax.rem(z + d, ZS) * XS for d in range(ZS)]
    xs = [lax.rem(x + d, XS) for d in range(XS)]
    order = sorted(
        (-hops_of(dy, dz, dx), dy, dz, dx) for dy in range(YS) for dz in range(ZS) for dx in range(XS)
    )
    return [ys[dy] + zs[dz] + xs[dx] for hops, dy, dz, dx in order if hops]


def far_first_of(y, z, x, parity):
    ys = [lax.rem(y + d, YS) * (ZS * XS) for d in range(YS)]
    xs = [lax.rem(x + d, XS) for d in range(XS)]
    same = lax.rem(z, 2) == parity
    steps = ((4, 3), (2, 5), (6, 1), (0, 7))
    zs = [lax.rem(z + jnp.where(same, even, odd), ZS) * XS for even, odd in steps]
    order = sorted(
        (-hops_of(dy, even, dx) - hops_of(dy, odd, dx), dy, n, dx)
        for dy in range(YS)
        for n, (even, odd) in enumerate(steps)
        for dx in range(XS)
    )
    assert order[-1][1:] == (0, 3, 0)
    return [ys[dy] + zs[n] + xs[dx] for hops, dy, n, dx in order]


def kernel(
    mode_hbm, levels_hbm, jitter_hbm, offsets_hbm, scat_hbm,
    dens_ref, pol_ref,
    mode, levels, jitter, offsets,
    raw_in, lev_out, lev_in, spec, spec_in, en_row, en_in, occ_all, dens_out, d_all, h_all, pol_out, pol_in,
    go, load_sem, raw_send, raw_recv, lev_send, lev_recv, en_send, en_recv, occ_send, occ_recv,
    spec_send, spec_recv, dens_send, dens_recv, pol_send, pol_recv,
):
    s = lax.axis_index("slab")
    e = lax.axis_index("energy")
    y = e // (ZS * XS)
    z = lax.rem(e // XS, ZS)
    x = lax.rem(e, XS)
    me = s * ENERGY + e
    half = 16

    barrier = pltpu.get_barrier_semaphore()
    level_load = pltpu.make_async_copy(levels_hbm, levels, load_sem.at[0])

    def remote(src, dst, send, recv, device):
        return pltpu.make_async_remote_copy(
            src_ref=src, dst_ref=dst, send_sem=send, recv_sem=recv, device_id=device, device_id_type=LOGICAL
        )

    def raw_copy(hub, h):
        return remote(
            scat_hbm.at[:, :, pl.ds(half * hub + 8 * h, 8), :], raw_in.at[s, h],
            raw_send.at[hub, h], raw_recv.at[s, h], hub * ENERGY + e,
        )

    def lev_copy(hub):
        return remote(lev_out, lev_in.at[s], lev_send.at[hub], lev_recv.at[s], hub * ENERGY + e)

    def load_levels():
        level_load.wait()
        for i in range(2):
            level = jnp.full((1, 128), levels[i], jnp.int32)
            lev_out[i : i + 1, :] = STEP_V * level.astype(jnp.float32)

    def all_pol(count):
        return remote(pol_in.at[pl.ds(0, count)], pol_in.at[pl.ds(0, count)], pol_send, pol_recv, me)

    @pl.when(s >= HUBS)
    def _():
        level_load.start()
        pl.semaphore_wait(barrier, HUBS)
        for hub in range(HUBS):

            @pl.when(s == HUBS)
            def _():
                pl.semaphore_signal(go, 1, device_id=hub * ENERGY + e, device_id_type=LOGICAL)

        for h in range(2):
            for hub in range(HUBS):
                raw_copy(hub, h).start()
        load_levels()
        for hub in range(HUBS):
            lev_copy(hub).start()
        for hub in range(HUBS):
            for h in range(2):
                raw_copy(hub, h).wait_send()
            lev_copy(hub).wait_send()
            remote(
                dens_out.at[0], dens_ref.at[:, pl.ds(2 * hub, 2)],
                dens_send.at[0], dens_recv.at[hub], me,
            ).wait_recv()
        all_pol(SENDERS).wait_recv()

    @pl.when(s < HUBS)
    def _():
        other = HUBS - 1 - s
        for leaf in range(HUBS, SLABS):
            pl.semaphore_signal(barrier, 1, device_id=leaf * ENERGY + e, device_id_type=LOGICAL)
        peers = far_first(y, z, x)
        for peer in peers:
            pl.semaphore_signal(barrier, 1, device_id=s * ENERGY + peer, device_id_type=LOGICAL)

        loads = [
            pltpu.make_async_copy(jitter_hbm, jitter, load_sem.at[1]),
            pltpu.make_async_copy(mode_hbm.at[pl.ds(8 * s, 8)], mode, load_sem.at[2]),
            pltpu.make_async_copy(offsets_hbm, offsets, load_sem.at[3]),
        ] + [
            pltpu.make_async_copy(
                scat_hbm.at[:, :, pl.ds(half * s + 8 * h, 8), :], raw_in.at[s, h], load_sem.at[4 + h]
            )
            for h in range(2)
        ]
        level_load.start()
        for copy in loads:
            copy.start()
        load_levels()
        lev_in[s] = lev_out[...]
        for copy in loads:
            copy.wait()

        odd = lax.rem(lax.broadcasted_iota(jnp.int32, (8, 128), 0), 2) == 1
        lane = lax.broadcasted_iota(jnp.int32, (8, 128), 1)
        energy = []
        for i in range(2):
            fine = jnp.full((8, 128), FINE * (2 * e + i) + jitter[i], jnp.int32)
            energy.append(E_LOW + E_SPAN * fine.astype(jnp.float32) / (FINE * POINTS))
        own_energy = jnp.where(odd, energy[1], energy[0])
        own_occ = 1.0 / (1.0 + jnp.exp(own_energy / KT))
        place = lane // 16
        mine = jnp.where(place == 2 * x, energy[0], jnp.where(place == 2 * x + 1, energy[1], 0.0))
        en_row[...] = mine[0:1, :]

        pl.semaphore_wait(go, 1)
        for h in range(2):
            raw_copy(other, h).start()
        lev_copy(other).start()

        base = []
        for h in range(2):
            modes = [
                jnp.broadcast_to(mode[4 * h + q : 4 * h + q + 1, :], (2, 128)) for q in range(4)
            ]
            base.append(own_energy - jnp.concatenate(modes, axis=0))

        def wait_levels(source):
            remote(lev_out, lev_in.at[source], lev_send.at[0], lev_recv.at[source], me).wait_recv()

        def wait_raw(source, h):
            remote(
                raw_in.at[source, h], raw_in.at[source, h], raw_send.at[0, 0], raw_recv.at[source, h], me
            ).wait_recv()

        def coefficients(source, h):
            part = [interleave(raw_in[source, h, c, 0], raw_in[source, h, c, 1], odd) for c in range(2)]
            return [
                (base[h] - lev_in[source, k : k + 1, :] - part[0][k], ETA - part[1][k]) for k in range(2)
            ]

        wait_levels(other)
        one = jnp.full((8, 128), 1.0, jnp.float32)
        zero = jnp.zeros((8, 128), jnp.float32)
        contact = (zero, jnp.full((8, 128), -GAMMA, jnp.float32))
        early, theta = [], []
        for h in range(2):
            wait_raw(other, h)
            a = coefficients(0, h) + coefficients(1, h)
            chain = [contact, (one, zero), (a[0][0], a[0][1] + GAMMA)]
            for layer in range(1, 4):
                chain.append(step(a[layer], chain[-1], chain[-2]))
            early.append(a)
            theta.append(chain[1:])

        block = lax.rem(e, BLOCKS)
        def send_energies():
            for peer in peers:
                remote(en_row, en_in.at[e], en_send, en_recv, s * ENERGY + peer).start()

        pl.semaphore_wait(barrier, ENERGY - 1)

        @pl.when(s == 0)
        def _():
            send_energies()

        en_in[e] = en_row[...]

        for h in range(2):
            for leaf in range(HUBS, SLABS):
                if h == 0:
                    wait_levels(leaf)
                wait_raw(leaf, h)
            a = early[h] + coefficients(2, h) + coefficients(3, h)
            left = list(theta[h])
            for layer in range(4, LAYERS - 1):
                left.append(step(a[layer], left[-1], left[-2]))
            right = [(one, zero), (a[LAYERS - 1][0], a[LAYERS - 1][1] + GAMMA)]
            for layer in reversed(range(1, LAYERS - 1)):
                right.append(step(a[layer], right[-1], right[-2]))
            det = step(a[4], times(left[4], right[3]), times(left[3], right[3]))
            tail = times(left[4], right[2])
            det = (det[0] - tail[0], det[1] - tail[1])
            scale = 2.0 / (det[0] * det[0] + det[1] * det[1])
            weight = (-det[0] * scale, det[1] * scale)
            density = []
            for layer in range(LAYERS):
                product = times(left[layer], right[LAYERS - 1 - layer])
                spectral = product[0] * weight[1] + product[1] * weight[0]
                density.append(own_occ * spectral)
                for q in range(4):
                    spec[8 * layer + 4 * h + q] = spectral[2 * q : 2 * q + 2, :]


            def send_spec(peer):
                remote(
                    spec.at[lax.rem(peer, BLOCKS)], spec_in.at[e], spec_send, spec_recv, s * ENERGY + peer
                ).start()

            group = far_first_of(y, z, x, h)
            for peer in group[:-1]:
                send_spec(peer)
            nearest = group[-1]

            @pl.when(nearest != e)
            def _():
                send_spec(nearest)

            for t in range(SLABS):
                first, second = interleave(density[2 * t], density[2 * t + 1], odd)
                dens_out[t, 0, h] = first
                dens_out[t, 1, h] = second
        spec_in[e] = spec[block]

        def dens_copy(target):
            return remote(
                dens_out.at[target], dens_ref.at[:, pl.ds(2 * s, 2)],
                dens_send.at[target], dens_recv.at[s], target * ENERGY + e,
            )

        dens_copy(other).start()
        for leaf in range(HUBS, SLABS):
            dens_copy(leaf).start()
        dens_ref[:, pl.ds(2 * s, 2)] = dens_out[s]

        occ_copy = remote(occ_all, occ_all, occ_send, occ_recv, other * ENERGY + e)

        @pl.when(s == 0)
        def _():
            remote(
                en_in.at[pl.ds(0, ENERGY - 1)], en_in.at[pl.ds(0, ENERGY - 1)], en_send, en_recv, me
            ).wait()
            diagonal = place == lax.broadcasted_iota(jnp.int32, (8, 128), 0)
            for i in range(ROWS):
                together = (en_in[4 * i] + en_in[4 * i + 1]) + (en_in[4 * i + 2] + en_in[4 * i + 3])
                spread = jnp.where(diagonal, jnp.broadcast_to(together, (8, 128)), -100.0)
                column = jnp.broadcast_to(jnp.max(spread, axis=1, keepdims=True), (8, 128))
                occ_all[8 * i : 8 * i + 8, :] = 1.0 / (1.0 + jnp.exp(column / KT))
            occ_copy.start()

        @pl.when(s == 1)
        def _():
            occ_copy.wait_recv()

        spec_all = remote(
            spec_in.at[pl.ds(0, ENERGY - 1)], spec_in.at[pl.ds(0, ENERGY - 1)], spec_send, spec_recv, me
        )
        spec_all.wait()
        spectra = spec_in[...].reshape(POINTS, 128)
        occ = occ_all[...]
        holes = (1.0 - occ) * spectra
        h_all[0:POINTS, :] = holes
        h_all[POINTS : 2 * POINTS, :] = holes
        d_all[...] = occ * spectra
        d = [d_all[8 * t : 8 * t + 8, :] for t in range(POINTS // 8)]

        first_offset = e - block
        high = lax.rem(y, 2)
        layer = block // 8
        target = layer // 2
        slot = (s * 8 + lax.rem(block, 8)) * 2 + lax.rem(layer, 2)
        own = (target == s).astype(jnp.int32)

        def correlate(k):
            start = POINTS - offsets[first_offset + k]
            parts = []
            for t in range(POINTS // 8):
                term = d[t] * h_all[pl.ds(start + 8 * t, 8), :]
                if t < 2:
                    parts.append(term)
                else:
                    parts[t % 2] = parts[t % 2] + term
            total = parts[0] + parts[1]
            pol_out[k] = jnp.sum(total, axis=0, keepdims=True) * (1.0 / POINTS)

        def give(k):
            peer = target * ENERGY + first_offset + k
            remote(pol_out.at[k], pol_in.at[slot], pol_send, pol_recv, peer).start()

        def one_offset(i, carry):
            k = lax.rem(block + BLOCKS - 1 - i, BLOCKS)
            correlate(k)
            give(k)
            return carry

        lax.fori_loop(0, BLOCKS - 1, one_offset, 0, unroll=3)
        correlate(block)

        @pl.when(own == 0)
        def _():
            give(block)

        @pl.when(own == 1)
        def _():
            pol_in[slot] = pol_out[block]
            remote(
                pol_out.at[pl.ds(0, BLOCKS - 1)], pol_out.at[pl.ds(0, BLOCKS - 1)], pol_send, pol_recv, me
            ).wait_send()
            all_pol(SENDERS - 1).wait_recv()

        @pl.when(own == 0)
        def _():
            remote(pol_out, pol_out, pol_send, pol_recv, me).wait_send()
            all_pol(SENDERS).wait_recv()

        @pl.when(s == 0)
        def _():
            occ_copy.wait_send()

        dens_copy(other).wait_send()
        for leaf in range(HUBS, SLABS):
            dens_copy(leaf).wait_send()
        remote(
            dens_out.at[0], dens_ref.at[:, pl.ds(2 * other, 2)], dens_send.at[0], dens_recv.at[other], me
        ).wait_recv()
        for h in range(2):
            raw_copy(other, h).wait_send()
        lev_copy(other).wait_send()

    for m in range(16):
        for k in range(2):
            pol_ref[m, k : k + 1, :] = pol_in[2 * m + k]


def write_out(dens_ref, pol_ref, dens_hbm, pol_hbm, sem):
    copies = [
        pltpu.make_async_copy(dens_ref, dens_hbm, sem.at[0]),
        pltpu.make_async_copy(pol_ref, pol_hbm, sem.at[1]),
    ]
    for copy in copies:
        copy.start()
    for copy in copies:
        copy.wait()


def local(mode_energy, levels, energy_jitter, offsets, scattering):
    modes = mode_energy.reshape(16, 128)
    scat = scattering.reshape(2, 2, 2, 16, 128).transpose(0, 1, 3, 2, 4).reshape(2, 2, 32, 128)
    f32 = jnp.float32
    dma = pltpu.SemaphoreType.DMA
    hbm = pl.BlockSpec(memory_space=pl.ANY)
    vmem = pl.BlockSpec(memory_space=pltpu.VMEM)
    density, polarization = pl.pallas_call(
        kernel,
        out_shape=(
            pltpu.VMEM((2, SLABS, 8, 128), f32),
            pltpu.VMEM((16, 2, 128), f32),
        ),
        in_specs=[hbm] * 5,
        out_specs=(vmem, vmem),
        scratch_shapes=[
            pltpu.VMEM((8, 128), f32),
            pltpu.SMEM((2,), jnp.int32),
            pltpu.SMEM((2,), jnp.int32),
            pltpu.SMEM((128,), jnp.int32),
            pltpu.VMEM((SLABS, 2, 2, 2, 8, 128), f32),
            pltpu.VMEM((2, 128), f32),
            pltpu.VMEM((SLABS, 2, 128), f32),
            pltpu.VMEM((BLOCKS, 2, 128), f32),
            pltpu.VMEM((ENERGY, 2, 128), f32),
            pltpu.VMEM((1, 128), f32),
            pltpu.VMEM((ENERGY, 1, 128), f32),
            pltpu.VMEM((POINTS, 128), f32),
            pltpu.VMEM((SLABS, 2, 2, 8, 128), f32),
            pltpu.VMEM((POINTS, 128), f32),
            pltpu.VMEM((2 * POINTS, 128), f32),
            pltpu.VMEM((BLOCKS, 1, 128), f32),
            pltpu.VMEM((SENDERS, 1, 128), f32),
            pltpu.SemaphoreType.REGULAR,
            dma((6,)),
            dma((HUBS, 2)),
            dma((SLABS, 2)),
            dma((HUBS,)),
            dma((SLABS,)),
            dma,
            dma,
            dma,
            dma,
            dma,
            dma,
            dma((SLABS,)),
            dma((HUBS,)),
            dma,
            dma,
        ],
        compiler_params=pltpu.CompilerParams(collective_id=0, has_side_effects=True),
        name="green_polarization",
    )(modes, levels, energy_jitter, offsets, scat)
    density, polarization = pl.pallas_call(
        write_out,
        out_shape=(
            jax.ShapeDtypeStruct((2, SLABS, 8, 128), f32),
            jax.ShapeDtypeStruct((16, 2, 128), f32),
        ),
        in_specs=[vmem] * 2,
        out_specs=(hbm, hbm),
        scratch_shapes=[dma((2,))],
        name="write_out",
    )(
        pltpu.with_memory_space_constraint(density, pltpu.VMEM),
        pltpu.with_memory_space_constraint(polarization, pltpu.VMEM),
    )
    density = density.reshape(2, 16, 2, 128).transpose(0, 2, 1, 3).reshape(2, 2, 2048)
    polarization = polarization.transpose(1, 0, 2).reshape(1, 2, 2048)
    return density, polarization


def solution(mesh):
    placed = (P(), P("slab"), P("energy"), P(), P(None, "energy", "slab", None))
    return jax.shard_map(
        local,
        mesh=mesh,
        in_specs=placed,
        out_specs=(P("energy", "slab", None), P("energy", "slab", None)),
        check_vma=False,
    )
```

```python
import jax
import jax.numpy as jnp
from jax import lax
from jax.experimental import pallas as pl
from jax.experimental.pallas import tpu as pltpu
from jax.sharding import PartitionSpec as P

FINE = 8
ETA = 0.1
GAMMA = 0.5
KT = 0.25
STEP_V = 0.15
E_LOW = -3.0
E_SPAN = 6.0

SLABS = 4
HUBS = 2
YS, ZS, XS = 4, 8, 4
ENERGY = YS * ZS * XS
ROWS = YS * ZS
POINTS = 256
LAYERS = 8
BLOCKS = 64
SENDERS = 32
LOGICAL = pl.DeviceIdType.LOGICAL


def times(p, q):
    return p[0] * q[0] - p[1] * q[1], p[0] * q[1] + p[1] * q[0]


def step(a, near, far):
    product = times(a, near)
    return product[0] - far[0], product[1] - far[1]


def interleave(first, second, odd):
    return (
        jnp.where(odd, pltpu.roll(second, 1, 0), first),
        jnp.where(odd, second, pltpu.roll(first, 7, 0)),
    )


def hops_of(dy, dz, dx):
    return 2 * min(dy, YS - dy) + min(dz, ZS - dz) + min(dx, XS - dx)


def far_first(y, z, x):
    ys = [lax.rem(y + d, YS) * (ZS * XS) for d in range(YS)]
    zs = [lax.rem(z + d, ZS) * XS for d in range(ZS)]
    xs = [lax.rem(x + d, XS) for d in range(XS)]
    order = sorted(
        (-hops_of(dy, dz, dx), dy, dz, dx) for dy in range(YS) for dz in range(ZS) for dx in range(XS)
    )
    return [ys[dy] + zs[dz] + xs[dx] for hops, dy, dz, dx in order if hops]


def far_first_of(y, z, x, parity):
    ys = [lax.rem(y + d, YS) * (ZS * XS) for d in range(YS)]
    xs = [lax.rem(x + d, XS) for d in range(XS)]
    same = lax.rem(z, 2) == parity
    steps = ((4, 3), (2, 5), (6, 1), (0, 7))
    zs = [lax.rem(z + jnp.where(same, even, odd), ZS) * XS for even, odd in steps]
    order = sorted(
        (-hops_of(dy, even, dx) - hops_of(dy, odd, dx), dy, n, dx)
        for dy in range(YS)
        for n, (even, odd) in enumerate(steps)
        for dx in range(XS)
    )
    assert order[-1][1:] == (0, 3, 0)
    return [ys[dy] + zs[n] + xs[dx] for hops, dy, n, dx in order]


def kernel(
    mode_hbm, levels_hbm, jitter_hbm, offsets_hbm, scat_hbm,
    dens_ref, pol_ref,
    mode, levels, jitter, offsets,
    raw_in, lev_out, lev_in, spec, spec_in, en_row, en_in, occ_all, dens_out, d_all, h_all, pol_out, pol_in,
    go, load_sem, raw_send, raw_recv, lev_send, lev_recv, en_send, en_recv, occ_send, occ_recv,
    spec_send, spec_recv, dens_send, dens_recv, pol_send, pol_recv,
):
    s = lax.axis_index("slab")
    e = lax.axis_index("energy")
    y = e // (ZS * XS)
    z = lax.rem(e // XS, ZS)
    x = lax.rem(e, XS)
    me = s * ENERGY + e
    half = 16

    barrier = pltpu.get_barrier_semaphore()
    level_load = pltpu.make_async_copy(levels_hbm, levels, load_sem.at[0])

    def remote(src, dst, send, recv, device):
        return pltpu.make_async_remote_copy(
            src_ref=src, dst_ref=dst, send_sem=send, recv_sem=recv, device_id=device, device_id_type=LOGICAL
        )

    def raw_copy(hub, h):
        return remote(
            scat_hbm.at[:, :, pl.ds(half * hub + 8 * h, 8), :], raw_in.at[s, h],
            raw_send.at[hub, h], raw_recv.at[s, h], hub * ENERGY + e,
        )

    def lev_copy(hub):
        return remote(lev_out, lev_in.at[s], lev_send.at[hub], lev_recv.at[s], hub * ENERGY + e)

    def load_levels():
        level_load.wait()
        for i in range(2):
            level = jnp.full((1, 128), levels[i], jnp.int32)
            lev_out[i : i + 1, :] = STEP_V * level.astype(jnp.float32)

    def all_pol(count):
        return remote(pol_in.at[pl.ds(0, count)], pol_in.at[pl.ds(0, count)], pol_send, pol_recv, me)

    @pl.when(s >= HUBS)
    def _():
        level_load.start()
        pl.semaphore_wait(barrier, HUBS)
        for hub in range(HUBS):

            @pl.when(s == HUBS)
            def _():
                pl.semaphore_signal(go, 1, device_id=hub * ENERGY + e, device_id_type=LOGICAL)

        for h in range(2):
            for hub in range(HUBS):
                raw_copy(hub, h).start()
        load_levels()
        for hub in range(HUBS):
            lev_copy(hub).start()
        for hub in range(HUBS):
            for h in range(2):
                raw_copy(hub, h).wait_send()
            lev_copy(hub).wait_send()
            remote(
                dens_out.at[0], dens_ref.at[:, pl.ds(2 * hub, 2)],
                dens_send.at[0], dens_recv.at[hub], me,
            ).wait_recv()
        all_pol(SENDERS).wait_recv()

    @pl.when(s < HUBS)
    def _():
        other = HUBS - 1 - s
        for leaf in range(HUBS, SLABS):
            pl.semaphore_signal(barrier, 1, device_id=leaf * ENERGY + e, device_id_type=LOGICAL)
        peers = far_first(y, z, x)
        for peer in peers:
            pl.semaphore_signal(barrier, 1, device_id=s * ENERGY + peer, device_id_type=LOGICAL)

        loads = [
            pltpu.make_async_copy(jitter_hbm, jitter, load_sem.at[1]),
            pltpu.make_async_copy(mode_hbm.at[pl.ds(8 * s, 8)], mode, load_sem.at[2]),
            pltpu.make_async_copy(offsets_hbm, offsets, load_sem.at[3]),
        ] + [
            pltpu.make_async_copy(
                scat_hbm.at[:, :, pl.ds(half * s + 8 * h, 8), :], raw_in.at[s, h], load_sem.at[4 + h]
            )
            for h in range(2)
        ]
        level_load.start()
        for copy in loads:
            copy.start()
        load_levels()
        lev_in[s] = lev_out[...]
        for copy in loads:
            copy.wait()

        odd = lax.rem(lax.broadcasted_iota(jnp.int32, (8, 128), 0), 2) == 1
        lane = lax.broadcasted_iota(jnp.int32, (8, 128), 1)
        energy = []
        for i in range(2):
            fine = jnp.full((8, 128), FINE * (2 * e + i) + jitter[i], jnp.int32)
            energy.append(E_LOW + E_SPAN * fine.astype(jnp.float32) / (FINE * POINTS))
        own_energy = jnp.where(odd, energy[1], energy[0])
        own_occ = 1.0 / (1.0 + jnp.exp(own_energy / KT))
        place = lane // 16
        mine = jnp.where(place == 2 * x, energy[0], jnp.where(place == 2 * x + 1, energy[1], 0.0))
        en_row[...] = mine[0:1, :]

        pl.semaphore_wait(go, 1)
        for h in range(2):
            raw_copy(other, h).start()
        lev_copy(other).start()

        base = []
        for h in range(2):
            modes = [
                jnp.broadcast_to(mode[4 * h + q : 4 * h + q + 1, :], (2, 128)) for q in range(4)
            ]
            base.append(own_energy - jnp.concatenate(modes, axis=0))

        def wait_levels(source):
            remote(lev_out, lev_in.at[source], lev_send.at[0], lev_recv.at[source], me).wait_recv()

        def wait_raw(source, h):
            remote(
                raw_in.at[source, h], raw_in.at[source, h], raw_send.at[0, 0], raw_recv.at[source, h], me
            ).wait_recv()

        def coefficients(source, h):
            part = [interleave(raw_in[source, h, c, 0], raw_in[source, h, c, 1], odd) for c in range(2)]
            return [
                (base[h] - lev_in[source, k : k + 1, :] - part[0][k], ETA - part[1][k]) for k in range(2)
            ]

        wait_levels(other)
        one = jnp.full((8, 128), 1.0, jnp.float32)
        zero = jnp.zeros((8, 128), jnp.float32)
        contact = (zero, jnp.full((8, 128), -GAMMA, jnp.float32))
        early, theta = [], []
        for h in range(2):
            wait_raw(other, h)
            a = coefficients(0, h) + coefficients(1, h)
            chain = [contact, (one, zero), (a[0][0], a[0][1] + GAMMA)]
            for layer in range(1, 4):
                chain.append(step(a[layer], chain[-1], chain[-2]))
            early.append(a)
            theta.append(chain[1:])

        block = lax.rem(e, BLOCKS)
        def send_energies():
            for peer in peers:
                remote(en_row, en_in.at[e], en_send, en_recv, s * ENERGY + peer).start()

        @pl.when(s == 0)
        def _():
            pl.semaphore_wait(barrier, ENERGY - 1)
            send_energies()

        en_in[e] = en_row[...]

        for h in range(2):
            for leaf in range(HUBS, SLABS):
                if h == 0:
                    wait_levels(leaf)
                wait_raw(leaf, h)
            a = early[h] + coefficients(2, h) + coefficients(3, h)
            left = list(theta[h])
            for layer in range(4, LAYERS - 1):
                left.append(step(a[layer], left[-1], left[-2]))
            right = [(one, zero), (a[LAYERS - 1][0], a[LAYERS - 1][1] + GAMMA)]
            for layer in reversed(range(1, LAYERS - 1)):
                right.append(step(a[layer], right[-1], right[-2]))
            det = step(a[4], times(left[4], right[3]), times(left[3], right[3]))
            tail = times(left[4], right[2])
            det = (det[0] - tail[0], det[1] - tail[1])
            scale = 2.0 / (det[0] * det[0] + det[1] * det[1])
            weight = (-det[0] * scale, det[1] * scale)
            density = []
            for layer in range(LAYERS):
                product = times(left[layer], right[LAYERS - 1 - layer])
                spectral = product[0] * weight[1] + product[1] * weight[0]
                density.append(own_occ * spectral)
                for q in range(4):
                    spec[8 * layer + 4 * h + q] = spectral[2 * q : 2 * q + 2, :]


            if h == 0:

                @pl.when(s == 1)
                def _():
                    pl.semaphore_wait(barrier, ENERGY - 1)

            def send_spec(peer):
                remote(
                    spec.at[lax.rem(peer, BLOCKS)], spec_in.at[e], spec_send, spec_recv, s * ENERGY + peer
                ).start()

            group = far_first_of(y, z, x, h)
            for peer in group[:-1]:
                send_spec(peer)
            nearest = group[-1]

            @pl.when(nearest != e)
            def _():
                send_spec(nearest)

            for t in range(SLABS):
                first, second = interleave(density[2 * t], density[2 * t + 1], odd)
                dens_out[t, 0, h] = first
                dens_out[t, 1, h] = second
        spec_in[e] = spec[block]

        def dens_copy(target):
            return remote(
                dens_out.at[target], dens_ref.at[:, pl.ds(2 * s, 2)],
                dens_send.at[target], dens_recv.at[s], target * ENERGY + e,
            )

        dens_copy(other).start()
        for leaf in range(HUBS, SLABS):
            dens_copy(leaf).start()
        dens_ref[:, pl.ds(2 * s, 2)] = dens_out[s]

        occ_copy = remote(occ_all, occ_all, occ_send, occ_recv, other * ENERGY + e)

        @pl.when(s == 0)
        def _():
            remote(
                en_in.at[pl.ds(0, ENERGY - 1)], en_in.at[pl.ds(0, ENERGY - 1)], en_send, en_recv, me
            ).wait()
            diagonal = place == lax.broadcasted_iota(jnp.int32, (8, 128), 0)
            for i in range(ROWS):
                together = (en_in[4 * i] + en_in[4 * i + 1]) + (en_in[4 * i + 2] + en_in[4 * i + 3])
                spread = jnp.where(diagonal, jnp.broadcast_to(together, (8, 128)), -100.0)
                column = jnp.broadcast_to(jnp.max(spread, axis=1, keepdims=True), (8, 128))
                occ_all[8 * i : 8 * i + 8, :] = 1.0 / (1.0 + jnp.exp(column / KT))
            occ_copy.start()

        @pl.when(s == 1)
        def _():
            occ_copy.wait_recv()

        spec_all = remote(
            spec_in.at[pl.ds(0, ENERGY - 1)], spec_in.at[pl.ds(0, ENERGY - 1)], spec_send, spec_recv, me
        )
        spec_all.wait()
        spectra = spec_in[...].reshape(POINTS, 128)
        occ = occ_all[...]
        holes = (1.0 - occ) * spectra
        h_all[0:POINTS, :] = holes
        h_all[POINTS : 2 * POINTS, :] = holes
        d_all[...] = occ * spectra
        d = [d_all[8 * t : 8 * t + 8, :] for t in range(POINTS // 8)]

        first_offset = e - block
        high = lax.rem(y, 2)
        layer = block // 8
        target = layer // 2
        slot = (s * 8 + lax.rem(block, 8)) * 2 + lax.rem(layer, 2)
        own = (target == s).astype(jnp.int32)

        def correlate(k):
            start = POINTS - offsets[first_offset + k]
            parts = []
            for t in range(POINTS // 8):
                term = d[t] * h_all[pl.ds(start + 8 * t, 8), :]
                if t < 2:
                    parts.append(term)
                else:
                    parts[t % 2] = parts[t % 2] + term
            total = parts[0] + parts[1]
            pol_out[k] = jnp.sum(total, axis=0, keepdims=True) * (1.0 / POINTS)

        def give(k):
            peer = target * ENERGY + first_offset + k
            remote(pol_out.at[k], pol_in.at[slot], pol_send, pol_recv, peer).start()

        def one_offset(i, carry):
            k = lax.rem(block + BLOCKS - 1 - i, BLOCKS)
            correlate(k)
            give(k)
            return carry

        lax.fori_loop(0, BLOCKS - 1, one_offset, 0, unroll=9)
        correlate(block)

        @pl.when(own == 0)
        def _():
            give(block)

        @pl.when(own == 1)
        def _():
            pol_in[slot] = pol_out[block]
            remote(
                pol_out.at[pl.ds(0, BLOCKS - 1)], pol_out.at[pl.ds(0, BLOCKS - 1)], pol_send, pol_recv, me
            ).wait_send()
            all_pol(SENDERS - 1).wait_recv()

        @pl.when(own == 0)
        def _():
            remote(pol_out, pol_out, pol_send, pol_recv, me).wait_send()
            all_pol(SENDERS).wait_recv()

        @pl.when(s == 0)
        def _():
            occ_copy.wait_send()

        dens_copy(other).wait_send()
        for leaf in range(HUBS, SLABS):
            dens_copy(leaf).wait_send()
        remote(
            dens_out.at[0], dens_ref.at[:, pl.ds(2 * other, 2)], dens_send.at[0], dens_recv.at[other], me
        ).wait_recv()
        for h in range(2):
            raw_copy(other, h).wait_send()
        lev_copy(other).wait_send()

    for m in range(16):
        for k in range(2):
            pol_ref[m, k : k + 1, :] = pol_in[2 * m + k]


def write_out(dens_ref, pol_ref, dens_hbm, pol_hbm, sem):
    copies = [
        pltpu.make_async_copy(dens_ref, dens_hbm, sem.at[0]),
        pltpu.make_async_copy(pol_ref, pol_hbm, sem.at[1]),
    ]
    for copy in copies:
        copy.start()
    for copy in copies:
        copy.wait()


def local(mode_energy, levels, energy_jitter, offsets, scattering):
    modes = mode_energy.reshape(16, 128)
    scat = scattering.reshape(2, 2, 2, 16, 128).transpose(0, 1, 3, 2, 4).reshape(2, 2, 32, 128)
    f32 = jnp.float32
    dma = pltpu.SemaphoreType.DMA
    hbm = pl.BlockSpec(memory_space=pl.ANY)
    vmem = pl.BlockSpec(memory_space=pltpu.VMEM)
    density, polarization = pl.pallas_call(
        kernel,
        out_shape=(
            pltpu.VMEM((2, SLABS, 8, 128), f32),
            pltpu.VMEM((16, 2, 128), f32),
        ),
        in_specs=[hbm] * 5,
        out_specs=(vmem, vmem),
        scratch_shapes=[
            pltpu.VMEM((8, 128), f32),
            pltpu.SMEM((2,), jnp.int32),
            pltpu.SMEM((2,), jnp.int32),
            pltpu.SMEM((128,), jnp.int32),
            pltpu.VMEM((SLABS, 2, 2, 2, 8, 128), f32),
            pltpu.VMEM((2, 128), f32),
            pltpu.VMEM((SLABS, 2, 128), f32),
            pltpu.VMEM((BLOCKS, 2, 128), f32),
            pltpu.VMEM((ENERGY, 2, 128), f32),
            pltpu.VMEM((1, 128), f32),
            pltpu.VMEM((ENERGY, 1, 128), f32),
            pltpu.VMEM((POINTS, 128), f32),
            pltpu.VMEM((SLABS, 2, 2, 8, 128), f32),
            pltpu.VMEM((POINTS, 128), f32),
            pltpu.VMEM((2 * POINTS, 128), f32),
            pltpu.VMEM((BLOCKS, 1, 128), f32),
            pltpu.VMEM((SENDERS, 1, 128), f32),
            pltpu.SemaphoreType.REGULAR,
            dma((6,)),
            dma((HUBS, 2)),
            dma((SLABS, 2)),
            dma((HUBS,)),
            dma((SLABS,)),
            dma,
            dma,
            dma,
            dma,
            dma,
            dma,
            dma((SLABS,)),
            dma((HUBS,)),
            dma,
            dma,
        ],
        compiler_params=pltpu.CompilerParams(collective_id=0, has_side_effects=True),
        name="green_polarization",
    )(modes, levels, energy_jitter, offsets, scat)
    density, polarization = pl.pallas_call(
        write_out,
        out_shape=(
            jax.ShapeDtypeStruct((2, SLABS, 8, 128), f32),
            jax.ShapeDtypeStruct((16, 2, 128), f32),
        ),
        in_specs=[vmem] * 2,
        out_specs=(hbm, hbm),
        scratch_shapes=[dma((2,))],
        name="write_out",
    )(
        pltpu.with_memory_space_constraint(density, pltpu.VMEM),
        pltpu.with_memory_space_constraint(polarization, pltpu.VMEM),
    )
    density = density.reshape(2, 16, 2, 128).transpose(0, 2, 1, 3).reshape(2, 2, 2048)
    polarization = polarization.transpose(1, 0, 2).reshape(1, 2, 2048)
    return density, polarization


def solution(mesh):
    placed = (P(), P("slab"), P("energy"), P(), P(None, "energy", "slab", None))
    return jax.shard_map(
        local,
        mesh=mesh,
        in_specs=placed,
        out_specs=(P("energy", "slab", None), P("energy", "slab", None)),
        check_vma=False,
    )
```
